256 devices in a mesh: dp: 32 (over x, z), ctx: 8 (over y, core).
Axes of the slice: x: 4, y: 4, z: 8, core: 2. Of those that a mesh axis runs over, the one named last changes fastest.
Arguments:
- gen_rows: bfloat16 [65536, 5120], P(('dp', 'ctx')), may hold values from -6 to 6
- gen_queries: bfloat16 [65536, 2560], P(('dp', 'ctx')), may hold values from -400 to 400
- place: int32 [65536], P(('dp', 'ctx')), may hold values from 0 to 65535, as said below
- segment: int32 [32, 2048], P('dp', 'ctx'), may hold values from 0 to 3, never falling along the last dimension, each value on 1 to 1024 neighbouring positions
- key_value_weight: bfloat16 [5120, 1024], P('dp'), may hold values from -0.078125 to 0.078125
- key_norm_gain: float32 [512], replicated, may hold values from 0.1 to 1.9
Outputs:
- attended: bfloat16 [65536, 2560], P(('dp', 'ctx'))
The draws below stay inside these ranges and needn't reach their ends.
Inputs may be any that keep to these rules, and one draw needn't show every extreme that they name: `place`: each trainer row appears exactly once. A generated row held by the device at dp index s and ctx index c goes to a trainer row of the block (d * 8 + c) * 256 to (d * 8 + c + 1) * 256 - 1 for some d. At most 16 rows of one device go to one dp index d, and in every draw some devices send exactly 16 rows to some d.
All inputs are finite; a program needn't handle non-finite values.
Results may differ from the reference program's by a relative error of at most 0.011.
Values may be sent and summed in bfloat16 or wider, within the bound.
No kernel may reach another device: no remote copies, remote signals or barrier semaphores. Data moves between devices by JAX's collectives and lax.ppermute only.
A program may use at most 128 MiB of HBM per device.

```python
import math
import jax
import jax.numpy as jnp
import numpy as np
from jax import lax

MODEL_WIDTH = 5120
HEAD_SIZE = 128
QUERY_HEADS = 20
KEY_VALUE_HEADS = 4
GROUP = 4
LOC = 256
RANKS = 32
RANK_POSITIONS = 2048
TOKENS = 65536


def draw_gen_queries(key, part):
    key = jax.random.fold_in(key, 11)
    first = jax.random.fold_in(key, 0)
    base = jax.random.normal(first, (TOKENS, QUERY_HEADS * HEAD_SIZE), jnp.float32)
    value_states = jnp.clip(base, -6.0, 6.0)
    return value_states.astype(jnp.bfloat16)


def draw_place(key, part):
    key = jax.random.fold_in(key, 7)
    ranks = RANKS
    columns = RANK_POSITIONS // LOC
    mean_rows = LOC // ranks

    def column(sub, index):
        first, second, third = jax.random.split(sub, 3)
        offset = jax.random.randint(first, (), 0, ranks)
        labels = jax.random.permutation(second, ranks)
        source = jnp.arange(ranks)[:, None]
        target = jnp.arange(ranks)[None, :]
        differ = (target - source - offset) % ranks
        counts = mean_rows + mean_rows * (differ == 0).astype(jnp.int32) - mean_rows * (differ == 1).astype(jnp.int32)
        counts = counts[labels]
        ends = jnp.cumsum(counts, axis=0)
        position = jnp.arange(LOC)
        source_of = jnp.sum((position[None, None, :] >= ends[:, :, None]).astype(jnp.int32), axis=0)
        globals_rows = (jnp.arange(ranks)[:, None] * columns + index) * LOC + position[None, :]
        order = jnp.argsort(source_of.reshape(-1), stable=True)
        grouped = globals_rows.reshape(-1)[order].reshape(ranks, LOC)
        shuffles = jax.vmap(lambda k: jax.random.permutation(k, LOC))(jax.random.split(third, ranks))
        return jnp.take_along_axis(grouped, shuffles, axis=1)
    blocks = jax.vmap(column)(jax.random.split(key, columns), jnp.arange(columns))
    return jnp.transpose(blocks, (1, 0, 2)).reshape(TOKENS).astype(jnp.int32)


def steps_of(own_key, shape, cuts, smallest, top_value):
    level = 1.0
    for dim, blocks in cuts:
        draws = jax.random.uniform(jax.random.fold_in(jax.random.fold_in(own_key, 6), dim), (blocks,), jnp.float32, smallest / len(cuts), top_value / len(cuts))
        level = level * jnp.repeat(jnp.exp(draws), shape[dim] // blocks).reshape((-1,) + (1,) * (len(shape) - 1 - dim))
    return level


def length_profile(number_of, total, most, skew):
    portions = [(1 << 20) // math.isqrt(rank ** skew) + 1 for rank in range(2, number_of + 1)]
    rest, given = total - most - (number_of - 1), [1] * (number_of - 1)
    while rest > 0:
        candidates = [i for i in range(number_of - 1) if given[i] < most]
        mass, budget = sum([portions[i] for i in candidates]), rest
        for i in candidates:
            extra = min(most - given[i], max(1, budget * portions[i] // mass), rest)
            given[i] = given[i] + extra
            rest = rest - extra
    return np.array([most] + given)


def uneven(own_key, amount, total, bound, slope):
    if amount == 2:
        one = jax.random.randint(own_key, (), max(1, total - bound), min(bound, total - 1) + 1)
        return jnp.stack([one, total - one])
    sizes = jnp.asarray(length_profile(amount, total, bound, slope), jnp.int32)
    twos = (amount - 1) // 2
    donor, receiver = sizes[1:1 + 2 * twos:2], sizes[2:2 + 2 * twos:2]
    margin = jnp.minimum(donor - 1, bound - receiver)
    shifted = jax.random.randint(jax.random.fold_in(own_key, 1), (twos,), 0, 1 << 20) % (margin + 1)
    sizes = sizes.at[1:1 + 2 * twos:2].set(donor - shifted).at[2:2 + 2 * twos:2].set(receiver + shifted)
    return sizes[jax.random.permutation(jax.random.fold_in(own_key, 2), amount)]


def centred(own_key, dims, width, bound, cuts=(), kind=jnp.bfloat16):
    gain = steps_of(own_key, dims, cuts, -0.22, 0.18) if cuts else 1.0
    values = jax.random.normal(own_key, dims, jnp.float32) * width * gain
    return jnp.minimum(jnp.maximum(values, -bound), bound).astype(kind)


def setup_inputs(seed: int = 0) -> dict:
    arg_keys = jax.random.split(jax.random.key(seed), 7)
    return {
        "gen_rows": centred(arg_keys[0], (TOKENS, MODEL_WIDTH), 1.0, 6.0, ((0, 256),)),
        "gen_queries": draw_gen_queries(jax.random.fold_in(arg_keys[6], 71), 0),
        "place": draw_place(jax.random.fold_in(arg_keys[6], 71), 0),
        "segment": jax.vmap(lambda own: jnp.searchsorted(jnp.cumsum(uneven(own, GROUP, RANK_POSITIONS, RANK_POSITIONS // 2, 2)), jnp.arange(RANK_POSITIONS), side="right"))(jax.random.split(arg_keys[3], RANKS)).reshape((RANKS, RANK_POSITIONS)).astype(jnp.int32),
        "key_value_weight": centred(arg_keys[4], (MODEL_WIDTH, 2 * KEY_VALUE_HEADS * HEAD_SIZE), MODEL_WIDTH ** -0.5, 0.078125, ((0, 32),)),
        "key_norm_gain": jnp.clip(1.0 + 0.18 * jax.random.normal(arg_keys[5], (KEY_VALUE_HEADS * HEAD_SIZE,), jnp.float32), 0.1, 1.9),
    }


def attend_rank(args):
    query_rows, key_rows, value_states, seg = args
    head_groups = QUERY_HEADS // KEY_VALUE_HEADS
    queries_gathered = query_rows.astype(jnp.float32).reshape(RANK_POSITIONS, KEY_VALUE_HEADS, head_groups, HEAD_SIZE)
    keys_gathered = key_rows.astype(jnp.float32).reshape(RANK_POSITIONS, KEY_VALUE_HEADS, HEAD_SIZE)
    values_gathered = value_states.astype(jnp.float32).reshape(RANK_POSITIONS, KEY_VALUE_HEADS, HEAD_SIZE)
    scores = jnp.einsum('qhgd,khd->hgqk', queries_gathered, keys_gathered) * HEAD_SIZE ** (-0.5)
    where_pos = jnp.arange(RANK_POSITIONS)
    allowed = (where_pos[None, :] <= where_pos[:, None]) & (seg[None, :] == seg[:, None])
    masked = jnp.where(allowed, scores, jnp.float32(-1e+30))
    best_choice = lax.optimization_barrier(jnp.max(masked, axis=-1, keepdims=True))
    weights = jnp.where(allowed, jnp.exp(masked - best_choice), jnp.float32(0.0))
    total = lax.optimization_barrier(jnp.sum(weights, axis=-1))
    rounded = weights.astype(jnp.bfloat16).astype(jnp.float32)
    summed = jnp.einsum('hgqk,khd->qhgd', rounded, values_gathered)
    result = summed / jnp.transpose(total, (2, 0, 1))[..., None]
    return result.reshape(RANK_POSITIONS, QUERY_HEADS * HEAD_SIZE).astype(jnp.bfloat16)

def reference(gen_rows, gen_queries, place, segment, key_value_weight, key_norm_gain):
    rows = jnp.zeros((TOKENS, MODEL_WIDTH), jnp.bfloat16).at[place].set(gen_rows)
    query_rows = jnp.zeros((TOKENS, QUERY_HEADS * HEAD_SIZE), jnp.bfloat16).at[place].set(gen_queries)
    proj = jnp.dot(rows, key_value_weight, preferred_element_type=jnp.float32)
    row_width = KEY_VALUE_HEADS * HEAD_SIZE
    kraw = proj[:, :row_width]
    key_rows = kraw * lax.rsqrt(lax.optimization_barrier(jnp.mean(kraw * kraw, axis=-1, keepdims=True)) + 1e-06) * key_norm_gain
    key_rows = key_rows.astype(jnp.bfloat16)
    value_states = proj[:, row_width:].astype(jnp.bfloat16)
    out = lax.map(attend_rank, (query_rows.reshape(RANKS, RANK_POSITIONS, QUERY_HEADS * HEAD_SIZE), key_rows.reshape(RANKS, RANK_POSITIONS, row_width), value_states.reshape(RANKS, RANK_POSITIONS, row_width), segment))
    return out.reshape(TOKENS, QUERY_HEADS * HEAD_SIZE)
```

```python
import functools

import jax
import jax.numpy as jnp
from jax import lax
from jax.experimental import pallas as pl
from jax.experimental.pallas import tpu as pltpu
from jax.sharding import PartitionSpec as P

LOC = 256
RANKS = 32
CAPACITY = 16
SLOTS = RANKS * CAPACITY
WIDTH = 5120
HEAD_SIZE = 128
QUERY_HEADS = 20
KEY_VALUE_HEADS = 4
HEAD_GROUP = QUERY_HEADS // KEY_VALUE_HEADS
ROW_WIDTH = KEY_VALUE_HEADS * HEAD_SIZE
QUERY_WIDTH = QUERY_HEADS * HEAD_SIZE
RANK_POSITIONS = 2048
PAIR = 2 * LOC
REACH = 1024
WINDOW = REACH + LOC
SENT = PAIR + 16
SCORE_BASE2 = 1.4426950408889634 * HEAD_SIZE ** (-0.5)
BF16 = jnp.bfloat16
F32 = jnp.float32
PARAMS = dict(vmem_limit_bytes=48 << 20)


def whole(shape):
    return pl.BlockSpec(shape, lambda *_: (0,) * len(shape))


def iota(shape, dim):
    return lax.broadcasted_iota(jnp.int32, shape, dim)


def order_rows(col, row):
    same = (col // RANK_POSITIONS) == (row // RANK_POSITIONS)
    earlier = iota((LOC, LOC), 0) < iota((LOC, LOC), 1)
    order = jnp.sum((same & earlier).astype(jnp.int32), axis=0, keepdims=True)
    return row // RANK_POSITIONS, order


def order_cols(col, row):
    same = (col // RANK_POSITIONS) == (row // RANK_POSITIONS)
    earlier = iota((LOC, LOC), 1) < iota((LOC, LOC), 0)
    order = jnp.sum((same & earlier).astype(jnp.int32), axis=1, keepdims=True)
    return col // RANK_POSITIONS, order


def onehot(mask):
    return jnp.where(mask, F32(1), F32(0)).astype(BF16)


def pick(mask, values):
    return jnp.dot(onehot(mask), values, preferred_element_type=F32).astype(BF16)


def pack_queries_kernel(col_ref, row_ref, sib_col_ref, sib_row_ref, core_ref, q_ref, out_ref, code_ref):
    core = core_ref[0]
    target, order = order_rows(col_ref[...], row_ref[...])
    slot = target * CAPACITY + order
    out_ref[...] = pick(iota((SLOTS, LOC), 0) == slot, q_ref[...])

    @pl.when(pl.program_id(0) == 0)
    def _():
        code = jnp.zeros((8, 2 * SLOTS), F32)
        for col, row, k in ((col_ref, row_ref, core), (sib_col_ref, sib_row_ref, 1 - core)):
            target_c, order_c = order_cols(col[...], row[...])
            slot_c = target_c * (2 * CAPACITY) + k * CAPACITY + order_c
            hot = onehot(iota((LOC, 2 * SLOTS), 1) == slot_c)
            pos = jnp.broadcast_to(row[...] % LOC + 1, (8, LOC)).astype(F32).astype(BF16)
            code += jnp.dot(pos, hot, preferred_element_type=F32)
        code_ref[...] = code[0:1].astype(jnp.int32)


def pack_queries(col, row, sib_col, sib_row, core, queries):
    steps = 4
    width = QUERY_WIDTH // steps
    return pl.pallas_call(
        pack_queries_kernel,
        grid=(steps,),
        in_specs=[
            whole((LOC, 1)),
            whole((1, LOC)),
            whole((LOC, 1)),
            whole((1, LOC)),
            pl.BlockSpec(memory_space=pltpu.SMEM),
            pl.BlockSpec((LOC, width), lambda i: (0, i)),
        ],
        out_specs=[pl.BlockSpec((SLOTS, width), lambda i: (0, i)), whole((1, 2 * SLOTS))],
        out_shape=[
            jax.ShapeDtypeStruct((SLOTS, QUERY_WIDTH), BF16),
            jax.ShapeDtypeStruct((1, 2 * SLOTS), jnp.int32),
        ],
        compiler_params=pltpu.CompilerParams(**PARAMS),
        cost_estimate=pl.CostEstimate(
            flops=2 * SLOTS * LOC * QUERY_WIDTH, bytes_accessed=4 << 20, transcendentals=0
        ),
        name="pack_queries",
    )(col, row, sib_col, sib_row, core, queries)


def project_kernel(
    steps, col_ref, row_ref, sib_col_ref, sib_row_ref, core_ref, x_ref, sib_ref, w_ref, gain_ref, out_ref, acc
):
    step = pl.program_id(0)

    @pl.when(step == 0)
    def _():
        acc[...] = jnp.zeros_like(acc)

    acc[0:LOC, :] += jnp.dot(x_ref[...], w_ref[...], preferred_element_type=F32)
    acc[LOC:PAIR, :] += jnp.dot(sib_ref[...], w_ref[...], preferred_element_type=F32)

    @pl.when(step == steps - 1)
    def _():
        core = core_ref[0]
        is_key = core == 0
        raw = acc[...]
        level = lax.rsqrt(jnp.mean(raw * raw, axis=-1, keepdims=True) + 1e-06)
        level = jnp.where(is_key, level, F32(1))
        gain = jnp.where(is_key, gain_ref[...], F32(1))
        done = (raw * level * gain).astype(BF16)
        hots = []
        for col, row, k in ((col_ref, row_ref, core), (sib_col_ref, sib_row_ref, 1 - core)):
            target, order = order_rows(col[...], row[...])
            slot = target * (2 * CAPACITY) + k * CAPACITY + order
            hots.append(iota((2 * SLOTS, LOC), 0) == slot)
        out_ref[...] = pick(jnp.concatenate(hots, axis=1), done)


def project(col, row, sib_col, sib_row, core, rows, sib_rows, weight, gain):
    steps = 4
    depth = WIDTH // steps
    return pl.pallas_call(
        functools.partial(project_kernel, steps),
        grid=(steps,),
        in_specs=[
            whole((LOC, 1)),
            whole((1, LOC)),
            whole((LOC, 1)),
            whole((1, LOC)),
            pl.BlockSpec(memory_space=pltpu.SMEM),
            pl.BlockSpec((LOC, depth), lambda i: (0, i)),
            pl.BlockSpec((LOC, depth), lambda i: (0, i)),
            pl.BlockSpec((depth, ROW_WIDTH), lambda i: (i, 0)),
            whole((1, ROW_WIDTH)),
        ],
        out_specs=whole((2 * SLOTS, ROW_WIDTH)),
        out_shape=jax.ShapeDtypeStruct((2 * SLOTS, ROW_WIDTH), BF16),
        scratch_shapes=[pltpu.VMEM((PAIR, ROW_WIDTH), F32)],
        compiler_params=pltpu.CompilerParams(**PARAMS),
        cost_estimate=pl.CostEstimate(
            flops=2 * PAIR * WIDTH * ROW_WIDTH, bytes_accessed=12 << 20, transcendentals=0
        ),
        name="project",
    )(col, row, sib_col, sib_row, core, rows, sib_rows, weight, gain)


def unpack_kernel(code_ref, seg_ref, got_ref, out_ref):
    code = code_ref[...]
    half = (iota((1, 2 * SLOTS), 1) // CAPACITY) % 2
    where = jnp.where(code > 0, code - 1 + half * LOC, -1)
    out_ref[0:PAIR, :] = pick(iota((PAIR, 2 * SLOTS), 0) == where, got_ref[...])
    seg = jnp.broadcast_to(seg_ref[...], (16, PAIR))
    out_ref[PAIR:SENT, :] = seg.astype(F32).astype(BF16)


def unpack(code, seg, got):
    return pl.pallas_call(
        unpack_kernel,
        out_shape=jax.ShapeDtypeStruct((SENT, ROW_WIDTH), BF16),
        compiler_params=pltpu.CompilerParams(**PARAMS),
        cost_estimate=pl.CostEstimate(
            flops=2 * PAIR * 2 * SLOTS * ROW_WIDTH, bytes_accessed=2 << 20, transcendentals=0
        ),
        name="unpack",
    )(code, seg, got)


def attend_kernel(
    where_ref, code_ref, seg_ref, q_ref, a0, a1, a2, b0, b1, b2, out_ref, keys, values, bias, qs
):
    core = where_ref[0]
    ctx = where_ref[1]

    @pl.when(pl.program_id(0) == 0)
    def _():
        @pl.when(core == 0)
        def _():
            for dst, (s0, s1, s2) in ((keys, (a0, a1, a2)), (values, (b0, b1, b2))):
                dst[0:PAIR, :] = s2[0:PAIR, :]
                dst[PAIR : 2 * PAIR, :] = s1[0:PAIR, :]
                dst[2 * PAIR : WINDOW, :] = s0[0:LOC, :]

        @pl.when(core != 0)
        def _():
            for dst, (s0, s1, s2) in ((keys, (b0, b1, b2)), (values, (a0, a1, a2))):
                dst[0:LOC, :] = s2[LOC:PAIR, :]
                dst[LOC : LOC + PAIR, :] = s1[0:PAIR, :]
                dst[LOC + PAIR : WINDOW, :] = s0[0:PAIR, :]

        segs = [a[PAIR : PAIR + 16, :][0:1].astype(F32) for a in (a2, a1, a0)]
        left = jnp.concatenate([segs[0], segs[1], segs[2][:, 0:LOC]], axis=1)
        right = jnp.concatenate([segs[0][:, LOC:PAIR], segs[1], segs[2]], axis=1)
        key_seg = jnp.where(core == 0, left, right)
        query_seg = seg_ref[...].astype(F32)
        k = iota((LOC, WINDOW), 1)
        q = iota((LOC, WINDOW), 0)
        allowed = (k <= q + REACH) & (k >= REACH - ctx * LOC) & (key_seg == query_seg)
        bias[...] = jnp.where(allowed, F32(0), F32(-1e30))

    code = code_ref[...]
    qs[...] = pick(iota((LOC, SLOTS), 0) == code - 1, q_ref[...])
    head = pl.multiple_of(pl.program_id(0) * HEAD_SIZE, HEAD_SIZE)
    key_rows = keys[:, pl.ds(head, HEAD_SIZE)]
    value_rows = values[:, pl.ds(head, HEAD_SIZE)]
    for g in range(HEAD_GROUP):
        cols = slice(g * HEAD_SIZE, (g + 1) * HEAD_SIZE)
        scores = lax.dot_general(
            qs[:, cols], key_rows, (((1,), (1,)), ((), ())), preferred_element_type=F32
        )
        scores = scores + bias[...]
        best = jnp.max(scores, axis=-1, keepdims=True)
        p = jnp.exp2((scores - best) * SCORE_BASE2)
        total = jnp.sum(p, axis=-1, keepdims=True)
        summed = jnp.dot(p.astype(BF16), value_rows, preferred_element_type=F32)
        out_ref[:, cols] = (summed / total).astype(BF16)


def attend(where, code, seg_col, got_queries, mine, other):
    width = HEAD_GROUP * HEAD_SIZE
    block = whole((SENT, ROW_WIDTH))
    return pl.pallas_call(
        attend_kernel,
        grid=(KEY_VALUE_HEADS,),
        in_specs=[
            pl.BlockSpec(memory_space=pltpu.SMEM),
            whole((1, SLOTS)),
            whole((LOC, 1)),
            pl.BlockSpec((SLOTS, width), lambda i: (0, i)),
        ]
        + [block] * 6,
        out_specs=pl.BlockSpec((LOC, width), lambda i: (0, i)),
        out_shape=jax.ShapeDtypeStruct((LOC, QUERY_WIDTH), BF16),
        scratch_shapes=[
            pltpu.VMEM((WINDOW, ROW_WIDTH), BF16),
            pltpu.VMEM((WINDOW, ROW_WIDTH), BF16),
            pltpu.VMEM((LOC, WINDOW), F32),
            pltpu.VMEM((LOC, width), BF16),
        ],
        compiler_params=pltpu.CompilerParams(**PARAMS),
        cost_estimate=pl.CostEstimate(
            flops=4 * LOC * WINDOW * QUERY_WIDTH,
            bytes_accessed=8 << 20,
            transcendentals=LOC * WINDOW * QUERY_HEADS,
        ),
        name="attend",
    )(where, code, seg_col, got_queries, *mine, *other)


def swap_cores(array):
    return lax.ppermute(array, "ctx", [(i, i ^ 1) for i in range(8)])


def send_up(array, by):
    pairs = [(y * 2 + k, (y + by) * 2 + k) for y in range(4 - by) for k in range(2)]
    return lax.ppermute(array, "ctx", pairs)


def body(gen_rows, gen_queries, place, segment, key_value_weight, key_norm_gain):
    ctx = lax.axis_index("ctx")
    core = ctx % 2
    seg = segment.reshape(LOC)
    sib = swap_cores(jnp.stack([place, seg]))
    sib_rows = swap_cores(gen_rows)
    col, row = place.reshape(LOC, 1), place.reshape(1, LOC)
    sib_col, sib_row = sib[0].reshape(LOC, 1), sib[0].reshape(1, LOC)
    core_s = core.reshape(1)
    pair_seg = jnp.where(core == 0, jnp.concatenate([seg, sib[1]]), jnp.concatenate([sib[1], seg]))
    pair_seg = pair_seg.reshape(1, PAIR)

    query_slots, code = pack_queries(col, row, sib_col, sib_row, core_s, gen_queries)
    got_code = lax.all_to_all(
        code.reshape(RANKS, 2 * CAPACITY), "dp", split_axis=0, concat_axis=0, tiled=True
    )
    got_queries = lax.all_to_all(
        query_slots.reshape(RANKS, CAPACITY, QUERY_WIDTH), "dp", split_axis=0, concat_axis=0, tiled=True
    ).reshape(SLOTS, QUERY_WIDTH)

    half = lax.dynamic_slice_in_dim(key_value_weight, core * ROW_WIDTH, ROW_WIDTH, 1)
    weight = lax.all_gather(half, "dp", axis=0, tiled=True)
    slots = project(
        col, row, sib_col, sib_row, core_s, gen_rows, sib_rows, weight, key_norm_gain.reshape(1, ROW_WIDTH)
    )
    got = lax.all_to_all(
        slots.reshape(RANKS, 2 * CAPACITY, ROW_WIDTH), "dp", split_axis=0, concat_axis=0, tiled=True
    ).reshape(2 * SLOTS, ROW_WIDTH)
    mine0 = unpack(got_code.reshape(1, 2 * SLOTS), pair_seg, got)
    mine = [mine0, send_up(mine0, 1), send_up(mine0, 2)]
    other = [swap_cores(m) for m in mine]
    own_code = lax.dynamic_slice_in_dim(got_code, core * CAPACITY, CAPACITY, 1)
    where = jnp.stack([core, ctx])
    return attend(where, own_code.reshape(1, SLOTS), seg.reshape(LOC, 1), got_queries, mine, other)


def solution(mesh):
    placed = (
        P(("dp", "ctx"), None),
        P(("dp", "ctx"), None),
        P(("dp", "ctx")),
        P("dp", "ctx"),
        P("dp", None),
        P(),
    )
    return jax.shard_map(
        body, mesh=mesh, in_specs=placed, out_specs=P(("dp", "ctx"), None), check_vma=False
    )
```

```python
import functools

import jax
import jax.numpy as jnp
from jax import lax
from jax.experimental import pallas as pl
from jax.experimental.pallas import tpu as pltpu
from jax.sharding import PartitionSpec as P

LOC = 256
RANKS = 32
CAPACITY = 16
SLOTS = RANKS * CAPACITY
WIDTH = 5120
HEAD_SIZE = 128
QUERY_HEADS = 20
KEY_VALUE_HEADS = 4
HEAD_GROUP = QUERY_HEADS // KEY_VALUE_HEADS
ROW_WIDTH = KEY_VALUE_HEADS * HEAD_SIZE
QUERY_WIDTH = QUERY_HEADS * HEAD_SIZE
RANK_POSITIONS = 2048
PAIR = 2 * LOC
REACH = 1024
CODE_WIDTH = 128
NEAR = (0, -1, 1, -2)
RUN = WIDTH // 4
GROUP_WIDTH = HEAD_GROUP * HEAD_SIZE
EARLY = 2
WINDOW = REACH + LOC
SENT = PAIR + 16
SCORE_BASE2 = 1.4426950408889634 * HEAD_SIZE ** (-0.5)
BF16 = jnp.bfloat16
F32 = jnp.float32
PARAMS = dict(vmem_limit_bytes=60 << 20)


def whole(shape):
    return pl.BlockSpec(shape, lambda *_: (0,) * len(shape))


def iota(shape, dim):
    return lax.broadcasted_iota(jnp.int32, shape, dim)


def order_rows(col, row):
    same = (col // RANK_POSITIONS) == (row // RANK_POSITIONS)
    earlier = iota((LOC, LOC), 0) < iota((LOC, LOC), 1)
    order = jnp.sum((same & earlier).astype(jnp.int32), axis=0, keepdims=True)
    return row // RANK_POSITIONS, order


def order_cols(col, row):
    same = (col // RANK_POSITIONS) == (row // RANK_POSITIONS)
    earlier = iota((LOC, LOC), 1) < iota((LOC, LOC), 0)
    order = jnp.sum((same & earlier).astype(jnp.int32), axis=1, keepdims=True)
    return col // RANK_POSITIONS, order


def onehot(mask):
    return jnp.where(mask, F32(1), F32(0)).astype(BF16)


def pick(mask, values):
    return jnp.dot(onehot(mask), values, preferred_element_type=F32).astype(BF16)


def pack_queries_kernel(col_ref, row_ref, q_ref, early_ref, late_ref, hot):
    step = pl.program_id(0)

    @pl.when(step == 0)
    def _():
        target, order = order_rows(col_ref[...], row_ref[...])
        hot[...] = onehot(iota((SLOTS, LOC), 0) == target * CAPACITY + order)
        code = jnp.broadcast_to(col_ref[...] % LOC + 1, (LOC, CODE_WIDTH)).astype(F32).astype(BF16)
        early_ref[:, EARLY * GROUP_WIDTH :] = jnp.dot(
            hot[...], code, preferred_element_type=F32
        ).astype(BF16)

    packed = jnp.dot(hot[...], q_ref[...], preferred_element_type=F32).astype(BF16)
    for group in range(KEY_VALUE_HEADS):
        ref, first = (early_ref, 0) if group < EARLY else (late_ref, EARLY)

        @pl.when(step == group)
        def _(ref=ref, first=first, group=group):
            ref[:, (group - first) * GROUP_WIDTH : (group - first + 1) * GROUP_WIDTH] = packed


def pack_queries(col, row, queries):
    widths = (EARLY * GROUP_WIDTH + CODE_WIDTH, (KEY_VALUE_HEADS - EARLY) * GROUP_WIDTH)
    return pl.pallas_call(
        pack_queries_kernel,
        grid=(KEY_VALUE_HEADS,),
        in_specs=[
            whole((LOC, 1)),
            whole((1, LOC)),
            pl.BlockSpec((LOC, GROUP_WIDTH), lambda i: (0, i)),
        ],
        out_specs=[whole((SLOTS, w)) for w in widths],
        out_shape=[jax.ShapeDtypeStruct((SLOTS, w), BF16) for w in widths],
        scratch_shapes=[pltpu.VMEM((SLOTS, LOC), BF16)],
        compiler_params=pltpu.CompilerParams(**PARAMS),
        cost_estimate=pl.CostEstimate(
            flops=2 * SLOTS * LOC * QUERY_WIDTH, bytes_accessed=4 << 20, transcendentals=0
        ),
        name="pack_queries",
    )(col, row, queries)


def row_places_kernel(core_ref, col_ref, row_ref, sib_col_ref, sib_row_ref, out_ref):
    core = core_ref[0]
    for n, (col, row, k) in enumerate(((col_ref, row_ref, core), (sib_col_ref, sib_row_ref, 1 - core))):
        target, order = order_rows(col[...], row[...])
        slot = target * (2 * CAPACITY) + k * CAPACITY + order
        out_ref[:, n * LOC : (n + 1) * LOC] = onehot(iota((2 * SLOTS, LOC), 0) == slot)


def row_places(core, col, row, sib_col, sib_row):
    return pl.pallas_call(
        row_places_kernel,
        in_specs=[pl.BlockSpec(memory_space=pltpu.SMEM)] + [pl.BlockSpec(memory_space=pltpu.VMEM)] * 4,
        out_shape=jax.ShapeDtypeStruct((2 * SLOTS, PAIR), BF16),
        compiler_params=pltpu.CompilerParams(**PARAMS),
        cost_estimate=pl.CostEstimate(
            flops=2 * SLOTS * PAIR * 8, bytes_accessed=1 << 20, transcendentals=0
        ),
        name="row_places",
    )(core, col, row, sib_col, sib_row)


def project_kernel(
    table_ref, hot_ref, gain_ref, x_ref, sib_ref, w0, w1, w2, w3, out_ref, weight, acc, sems
):
    step = pl.program_id(0)
    core = table_ref[8]
    sources = (w0, w1, w2, w3)

    def copy(source, i, x, y):
        return pltpu.make_async_copy(
            source.at[pl.ds(i * RUN, RUN), :],
            weight.at[
                pl.ds(pl.multiple_of(x * RUN, RUN), RUN),
                pl.ds(pl.multiple_of(y * HEAD_SIZE, HEAD_SIZE), HEAD_SIZE),
            ],
            sems.at[x, y],
        )

    @pl.when(step == 0)
    def _():
        @pl.when(core == 0)
        def _():
            for i in range(4):
                for j in range(4):
                    copy(sources[j], i, table_ref[i], table_ref[4 + j]).start()

        @pl.when(core != 0)
        def _():
            for j in range(4):
                for i in range(4):
                    copy(sources[j], i, table_ref[j], table_ref[4 + i]).start()

    x = table_ref[step]
    for y in range(4):
        copy(w0, 0, x, y).wait()
    w = weight[pl.ds(pl.multiple_of(x * RUN, RUN), RUN), :]
    for n, ref in enumerate((x_ref, sib_ref)):
        now = jnp.dot(ref[...], w, preferred_element_type=F32)
        part = slice(n * LOC, (n + 1) * LOC)

        @pl.when(step == 0)
        def _(now=now, part=part):
            acc[part, :] = now

        @pl.when(step > 0)
        def _(now=now, part=part):
            acc[part, :] += now

    @pl.when(step == 3)
    def _():
        is_key = core == 0
        raw = acc[...]
        level = lax.rsqrt(jnp.mean(raw * raw, axis=-1, keepdims=True) + 1e-06)
        level = jnp.where(is_key, level, F32(1))
        gain = jnp.where(is_key, gain_ref[...], F32(1))
        done = (raw * level * gain).astype(BF16)
        out_ref[...] = jnp.dot(hot_ref[...], done, preferred_element_type=F32).astype(BF16)


def project(table, hot, gain, rows, sib_rows, weights):
    across = pl.BlockSpec((LOC, RUN), lambda t, table: (0, table[t]))
    return pl.pallas_call(
        project_kernel,
        grid_spec=pltpu.PrefetchScalarGridSpec(
            num_scalar_prefetch=1,
            grid=(4,),
            in_specs=[
                whole((2 * SLOTS, PAIR)),
                whole((1, ROW_WIDTH)),
                across,
                across,
            ]
            + [pl.BlockSpec(memory_space=pl.ANY)] * 4,
            out_specs=whole((2 * SLOTS, ROW_WIDTH)),
            scratch_shapes=[
                pltpu.VMEM((WIDTH, ROW_WIDTH), BF16),
                pltpu.VMEM((PAIR, ROW_WIDTH), F32),
                pltpu.SemaphoreType.DMA((4, 4)),
            ],
        ),
        out_shape=jax.ShapeDtypeStruct((2 * SLOTS, ROW_WIDTH), BF16),
        compiler_params=pltpu.CompilerParams(**PARAMS),
        cost_estimate=pl.CostEstimate(
            flops=2 * PAIR * WIDTH * ROW_WIDTH, bytes_accessed=12 << 20, transcendentals=0
        ),
        name="project",
    )(table, hot, gain, rows, sib_rows, *weights)


def places_kernel(core_ref, own_ref, sib_ref, out_ref):
    for n, code in enumerate((own_ref, sib_ref)):
        k = core_ref[0] if n == 0 else 1 - core_ref[0]
        row = code[...].astype(F32).T[0:1].astype(jnp.int32) - 1
        out_ref[k] = onehot(iota((LOC, SLOTS), 0) == row)


def places(core, own_code, sib_code):
    return pl.pallas_call(
        places_kernel,
        in_specs=[pl.BlockSpec(memory_space=pltpu.SMEM)] + [pl.BlockSpec(memory_space=pltpu.VMEM)] * 2,
        out_shape=jax.ShapeDtypeStruct((2, LOC, SLOTS), BF16),
        compiler_params=pltpu.CompilerParams(**PARAMS),
        cost_estimate=pl.CostEstimate(flops=SLOTS * LOC * 8, bytes_accessed=1 << 20, transcendentals=0),
        name="places",
    )(core, own_code, sib_code)


def unpack_queries_kernel(core_ref, hot_ref, q_ref, out_ref):
    out_ref[...] = jnp.dot(hot_ref[core_ref[0]], q_ref[...], preferred_element_type=F32).astype(BF16)


def unpack_queries(core, hots, got, groups):
    return pl.pallas_call(
        unpack_queries_kernel,
        grid=(groups,),
        in_specs=[
            pl.BlockSpec(memory_space=pltpu.SMEM),
            whole((2, LOC, SLOTS)),
            pl.BlockSpec((SLOTS, GROUP_WIDTH), lambda i: (0, i)),
        ],
        out_specs=pl.BlockSpec((LOC, GROUP_WIDTH), lambda i: (0, i)),
        out_shape=jax.ShapeDtypeStruct((LOC, groups * GROUP_WIDTH), BF16),
        compiler_params=pltpu.CompilerParams(**PARAMS),
        cost_estimate=pl.CostEstimate(
            flops=2 * SLOTS * LOC * groups * GROUP_WIDTH, bytes_accessed=4 << 20, transcendentals=0
        ),
        name="unpack_queries",
    )(core, hots, got)


def unpack_kernel(hot_ref, seg_ref, got_ref, out_ref):
    got = got_ref[...].reshape(RANKS, 2, CAPACITY, ROW_WIDTH)
    for k in range(2):
        part = got[:, k].reshape(SLOTS, ROW_WIDTH)
        out_ref[k * LOC : (k + 1) * LOC, :] = jnp.dot(
            hot_ref[k], part, preferred_element_type=F32
        ).astype(BF16)
    out_ref[PAIR:SENT, :] = jnp.broadcast_to(seg_ref[...].astype(F32).astype(BF16), (16, PAIR))


def unpack(hots, seg, got):
    return pl.pallas_call(
        unpack_kernel,
        out_shape=jax.ShapeDtypeStruct((SENT, ROW_WIDTH), BF16),
        compiler_params=pltpu.CompilerParams(**PARAMS),
        cost_estimate=pl.CostEstimate(
            flops=2 * PAIR * SLOTS * ROW_WIDTH, bytes_accessed=3 << 20, transcendentals=0
        ),
        name="unpack",
    )(hots, seg, got)


def attend_kernel(
    where_ref, seg_ref, early_ref, late_ref, a0, a1, a2, b0, b1, b2, out_ref, keys, values, bias, queries
):
    core = where_ref[0]
    ctx = where_ref[3]
    head = pl.program_id(0)

    @pl.when(head == 0)
    def _():
        @pl.when(core == 0)
        def _():
            for dst, (s0, s1, s2) in ((keys, (a0, a1, a2)), (values, (b0, b1, b2))):
                dst[0:PAIR, :] = s2[0:PAIR, :]
                dst[PAIR : 2 * PAIR, :] = s1[0:PAIR, :]
                dst[2 * PAIR : WINDOW, :] = s0[0:LOC, :]

        @pl.when(core != 0)
        def _():
            for dst, (s0, s1, s2) in ((keys, (b0, b1, b2)), (values, (a0, a1, a2))):
                dst[0:LOC, :] = s2[LOC:PAIR, :]
                dst[LOC : LOC + PAIR, :] = s1[0:PAIR, :]
                dst[LOC + PAIR : WINDOW, :] = s0[0:PAIR, :]

        segs = [a[PAIR:SENT, :][0:1].astype(F32) for a in (a2, a1, a0)]
        left = jnp.concatenate([segs[0], segs[1], segs[2][:, 0:LOC]], axis=1)
        right = jnp.concatenate([segs[0][:, LOC:PAIR], segs[1], segs[2]], axis=1)
        key_seg = jnp.where(core == 0, left, right)
        query_seg = seg_ref[...].astype(F32)
        k = iota((LOC, WINDOW), 1)
        q = iota((LOC, WINDOW), 0)
        allowed = (k <= q + REACH) & (k >= REACH - ctx * LOC) & (key_seg == query_seg)
        bias[...] = jnp.where(allowed, F32(0), F32(-1e30))

    @pl.when(head < EARLY)
    def _():
        queries[...] = early_ref[...]

    @pl.when(head >= EARLY)
    def _():
        queries[...] = late_ref[...]

    columns = pl.ds(pl.multiple_of(head * HEAD_SIZE, HEAD_SIZE), HEAD_SIZE)
    key_rows = keys[:, columns]
    value_rows = values[:, columns]
    value_rows = jnp.concatenate([value_rows, jnp.ones_like(value_rows)], axis=1)
    for g in range(HEAD_GROUP):
        cols = slice(g * HEAD_SIZE, (g + 1) * HEAD_SIZE)
        scores = lax.dot_general(
            queries[:, cols], key_rows, (((1,), (1,)), ((), ())), preferred_element_type=F32
        )
        scores = scores + bias[...]
        best = jnp.max(scores, axis=-1, keepdims=True)
        p = jnp.exp2((scores - best) * SCORE_BASE2).astype(BF16)
        summed = jnp.dot(p, value_rows, preferred_element_type=F32)
        out_ref[:, cols] = (summed[:, :HEAD_SIZE] / summed[:, HEAD_SIZE:]).astype(BF16)


def attend(where, seg_col, early, late, mine, other):
    return pl.pallas_call(
        attend_kernel,
        grid=(KEY_VALUE_HEADS,),
        in_specs=[
            pl.BlockSpec(memory_space=pltpu.SMEM),
            whole((LOC, 1)),
            pl.BlockSpec((LOC, GROUP_WIDTH), lambda i: (0, jnp.minimum(i, EARLY - 1))),
            pl.BlockSpec((LOC, GROUP_WIDTH), lambda i: (0, jnp.maximum(i - EARLY, 0))),
        ]
        + [whole((SENT, ROW_WIDTH))] * 6,
        out_specs=pl.BlockSpec((LOC, GROUP_WIDTH), lambda i: (0, i)),
        out_shape=jax.ShapeDtypeStruct((LOC, QUERY_WIDTH), BF16),
        scratch_shapes=[
            pltpu.VMEM((WINDOW, ROW_WIDTH), BF16),
            pltpu.VMEM((WINDOW, ROW_WIDTH), BF16),
            pltpu.VMEM((LOC, WINDOW), F32),
            pltpu.VMEM((LOC, GROUP_WIDTH), BF16),
        ],
        compiler_params=pltpu.CompilerParams(**PARAMS),
        cost_estimate=pl.CostEstimate(
            flops=4 * LOC * WINDOW * QUERY_WIDTH,
            bytes_accessed=8 << 20,
            transcendentals=LOC * WINDOW * QUERY_HEADS,
        ),
        name="attend",
    )(where, seg_col, early, late, *mine, *other)


def chips():
    return [(x, y, z, k) for x in range(4) for z in range(8) for y in range(4) for k in range(2)]


def device(x, y, z, k):
    return (x % 4 * 8 + z % 8) * 8 + y % 4 * 2 + k


def shift(array, moved):
    pairs = [(device(*c), device(*moved(*c))) for c in chips()]
    return lax.ppermute(array, ("dp", "ctx"), pairs)


def swap_cores(array):
    return shift(array, lambda x, y, z, k: (x, y, z, 1 - k))


def send_up(array, by):
    pairs = [(device(*c), device(c[0], c[1] + by, c[2], c[3])) for c in chips() if c[1] + by < 4]
    return lax.ppermute(array, ("dp", "ctx"), pairs)


def along_z(array):
    groups = [[device(x, y, z, k) for z in range(8)] for x in range(4) for y in range(4) for k in range(2)]
    copies = jnp.broadcast_to(array[None], (8,) + array.shape)
    got = lax.all_to_all(copies, ("dp", "ctx"), 0, 0, axis_index_groups=groups, tiled=True)
    return got.reshape(8 * array.shape[0], array.shape[1])


def along_first(array, by):
    return shift(array, lambda x, y, z, k: (x + by, y, z, k) if k == 0 else (x, y + by, z, k))


def along_second(array, by):
    return shift(array, lambda x, y, z, k: (x, y + by, z, k) if k == 0 else (x + by, y, z, k))


def move(slots, rows):
    width = slots.shape[1]
    sent = slots.reshape(RANKS, rows, width)
    return lax.all_to_all(sent, "dp", split_axis=0, concat_axis=0, tiled=True).reshape(RANKS * rows, width)


def body(gen_rows, gen_queries, place, segment, key_value_weight, key_norm_gain):
    ctx = lax.axis_index("ctx")
    core, chip_y = ctx % 2, ctx // 2
    chip_x = lax.axis_index("dp") // 8
    where = jnp.stack([core, chip_x, chip_y, ctx])
    core_s = core.reshape(1)
    seg = segment.reshape(LOC)
    col, row = place.reshape(LOC, 1), place.reshape(1, LOC)

    part = lax.dynamic_slice_in_dim(
        key_value_weight, core * ROW_WIDTH + chip_y * HEAD_SIZE, HEAD_SIZE, 1
    )
    run = along_z(part)
    early_slots, late_slots = pack_queries(col, row, gen_queries)
    line = jnp.concatenate([run] + [along_first(run, -by) for by in NEAR[1:]])
    early_slots, line = lax.optimization_barrier((early_slots, line))
    got_early = move(early_slots, CAPACITY)

    sib = swap_cores(jnp.stack([place, seg]))
    sib_rows = swap_cores(gen_rows)
    sib_col, sib_row = sib[0].reshape(LOC, 1), sib[0].reshape(1, LOC)
    pair_seg = jnp.where(core == 0, jnp.concatenate([seg, sib[1]]), jnp.concatenate([sib[1], seg]))
    pair_seg = pair_seg.reshape(1, PAIR)

    weights = [line] + [along_second(line, -by) for by in NEAR[1:]]
    hot = row_places(core_s, col, row, sib_col, sib_row)
    near = jnp.array(NEAR)
    table = jnp.concatenate([(chip_x + near) % 4, (chip_y + near) % 4, core_s])
    slots = project(table, hot, key_norm_gain.reshape(1, ROW_WIDTH), gen_rows, sib_rows, weights)
    slots, got_early = lax.optimization_barrier((slots, got_early))
    got = move(slots, 2 * CAPACITY)
    own_code = got_early[:, EARLY * GROUP_WIDTH :]
    hots = places(core_s, own_code, swap_cores(own_code))
    early = unpack_queries(core_s, hots, got_early, EARLY)
    got, early, hots = lax.optimization_barrier((got, early, hots))
    own = unpack(hots, pair_seg, got)
    late_slots, own = lax.optimization_barrier((late_slots, own))
    up = [send_up(own, 1), send_up(own, 2)]
    got_late = move(late_slots, CAPACITY)
    late = unpack_queries(core_s, hots, got_late, KEY_VALUE_HEADS - EARLY)
    other = [swap_cores(m) for m in [own] + up]
    return attend(where, seg.reshape(LOC, 1), early, late, [own] + up, other)


def solution(mesh):
    placed = (
        P(("dp", "ctx"), None),
        P(("dp", "ctx"), None),
        P(("dp", "ctx")),
        P("dp", "ctx"),
        P("dp", None),
        P(),
    )
    return jax.shard_map(
        body, mesh=mesh, in_specs=placed, out_specs=P(("dp", "ctx"), None), check_vma=False
    )
```

```python
import functools

import jax
import jax.numpy as jnp
from jax import lax
from jax.experimental import pallas as pl
from jax.experimental.pallas import tpu as pltpu
from jax.sharding import PartitionSpec as P

LOC = 256
RANKS = 32
CAPACITY = 16
SLOTS = RANKS * CAPACITY
WIDTH = 5120
HEAD_SIZE = 128
QUERY_HEADS = 20
KEY_VALUE_HEADS = 4
HEAD_GROUP = QUERY_HEADS // KEY_VALUE_HEADS
ROW_WIDTH = KEY_VALUE_HEADS * HEAD_SIZE
QUERY_WIDTH = QUERY_HEADS * HEAD_SIZE
RANK_POSITIONS = 2048
PAIR = 2 * LOC
REACH = 1024
CODE_WIDTH = 128
NEAR = (0, -1, 1, -2)
RUN = WIDTH // 4
GROUP_WIDTH = HEAD_GROUP * HEAD_SIZE
EARLY = 2
WINDOW = REACH + LOC
SENT = PAIR + 32
HALF = ROW_WIDTH // 2
SCORE_BASE2 = 1.4426950408889634 * HEAD_SIZE ** (-0.5)
BF16 = jnp.bfloat16
F32 = jnp.float32
PARAMS = dict(vmem_limit_bytes=24 << 20)


def whole(shape):
    return pl.BlockSpec(shape, lambda *_: (0,) * len(shape))


def iota(shape, dim):
    return lax.broadcasted_iota(jnp.int32, shape, dim)


def order_rows(col, row):
    same = (col // RANK_POSITIONS) == (row // RANK_POSITIONS)
    earlier = iota((LOC, LOC), 0) < iota((LOC, LOC), 1)
    order = jnp.sum((same & earlier).astype(jnp.int32), axis=0, keepdims=True)
    return row // RANK_POSITIONS, order


def order_cols(col, row):
    same = (col // RANK_POSITIONS) == (row // RANK_POSITIONS)
    earlier = iota((LOC, LOC), 1) < iota((LOC, LOC), 0)
    order = jnp.sum((same & earlier).astype(jnp.int32), axis=1, keepdims=True)
    return col // RANK_POSITIONS, order


def onehot(mask):
    return jnp.where(mask, F32(1), F32(0)).astype(BF16)


def pick(mask, values):
    return jnp.dot(onehot(mask), values, preferred_element_type=F32).astype(BF16)


def pack_queries_kernel(col_ref, row_ref, q_ref, early_ref, late_ref, hot):
    step = pl.program_id(0)

    @pl.when(step == 0)
    def _():
        target, order = order_rows(col_ref[...], row_ref[...])
        hot[...] = onehot(iota((SLOTS, LOC), 0) == target * CAPACITY + order)
        code = jnp.broadcast_to(col_ref[...] % LOC + 1, (LOC, CODE_WIDTH)).astype(F32).astype(BF16)
        early_ref[:, EARLY * GROUP_WIDTH :] = jnp.dot(
            hot[...], code, preferred_element_type=F32
        ).astype(BF16)

    packed = jnp.dot(hot[...], q_ref[...], preferred_element_type=F32).astype(BF16)
    for group in range(KEY_VALUE_HEADS):
        ref, first = (early_ref, 0) if group < EARLY else (late_ref, EARLY)

        @pl.when(step == group)
        def _(ref=ref, first=first, group=group):
            ref[:, (group - first) * GROUP_WIDTH : (group - first + 1) * GROUP_WIDTH] = packed


def pack_queries(col, row, queries):
    widths = (EARLY * GROUP_WIDTH + CODE_WIDTH, (KEY_VALUE_HEADS - EARLY) * GROUP_WIDTH)
    return pl.pallas_call(
        pack_queries_kernel,
        grid=(KEY_VALUE_HEADS,),
        in_specs=[
            whole((LOC, 1)),
            whole((1, LOC)),
            pl.BlockSpec((LOC, GROUP_WIDTH), lambda i: (0, i)),
        ],
        out_specs=[whole((SLOTS, w)) for w in widths],
        out_shape=[jax.ShapeDtypeStruct((SLOTS, w), BF16) for w in widths],
        scratch_shapes=[pltpu.VMEM((SLOTS, LOC), BF16)],
        compiler_params=pltpu.CompilerParams(**PARAMS),
        cost_estimate=pl.CostEstimate(
            flops=2 * SLOTS * LOC * QUERY_WIDTH, bytes_accessed=4 << 20, transcendentals=0
        ),
        name="pack_queries",
    )(col, row, queries)


def row_places_kernel(core_ref, col_ref, row_ref, sib_col_ref, sib_row_ref, out_ref):
    core = core_ref[0]
    for n, (col, row, k) in enumerate(((col_ref, row_ref, core), (sib_col_ref, sib_row_ref, 1 - core))):
        target, order = order_rows(col[...], row[...])
        slot = target * (2 * CAPACITY) + k * CAPACITY + order
        out_ref[:, n * LOC : (n + 1) * LOC] = onehot(iota((2 * SLOTS, LOC), 0) == slot)


def row_places(core, col, row, sib_col, sib_row):
    return pl.pallas_call(
        row_places_kernel,
        in_specs=[pl.BlockSpec(memory_space=pltpu.SMEM)] + [pl.BlockSpec(memory_space=pltpu.VMEM)] * 4,
        out_shape=jax.ShapeDtypeStruct((2 * SLOTS, PAIR), BF16),
        compiler_params=pltpu.CompilerParams(**PARAMS),
        cost_estimate=pl.CostEstimate(
            flops=2 * SLOTS * PAIR * 8, bytes_accessed=1 << 20, transcendentals=0
        ),
        name="row_places",
    )(core, col, row, sib_col, sib_row)


def project_kernel(
    table_ref, hot_ref, gain_ref, x_ref, sib_ref, *rest
):
    step = pl.program_id(0)
    core = table_ref[8]
    sources, (out_ref, weight, acc, sems) = rest[:8], rest[8:]

    def copy(j, i, x, y):
        return pltpu.make_async_copy(
            sources[2 * j + i // 2].at[pl.ds(i % 2 * RUN, RUN), :],
            weight.at[
                pl.ds(pl.multiple_of(x * RUN, RUN), RUN),
                pl.ds(pl.multiple_of(y * HEAD_SIZE, HEAD_SIZE), HEAD_SIZE),
            ],
            sems.at[x, y],
        )

    @pl.when(step == 0)
    def _():
        @pl.when(core == 0)
        def _():
            for i in range(4):
                for j in range(4):
                    copy(j, i, table_ref[i], table_ref[4 + j]).start()

        @pl.when(core != 0)
        def _():
            for j in range(4):
                for i in range(4):
                    copy(j, i, table_ref[j], table_ref[4 + i]).start()

    x = table_ref[step]
    for y in range(4):
        copy(0, 0, x, y).wait()
    w = weight[pl.ds(pl.multiple_of(x * RUN, RUN), RUN), :]
    for n, ref in enumerate((x_ref, sib_ref)):
        now = jnp.dot(ref[...], w, preferred_element_type=F32)
        part = slice(n * LOC, (n + 1) * LOC)

        @pl.when(step == 0)
        def _(now=now, part=part):
            acc[part, :] = now

        @pl.when(step > 0)
        def _(now=now, part=part):
            acc[part, :] += now

    @pl.when(step == 3)
    def _():
        is_key = core == 0
        raw = acc[...]
        level = lax.rsqrt(jnp.mean(raw * raw, axis=-1, keepdims=True) + 1e-06)
        level = jnp.where(is_key, level, F32(1))
        gain = jnp.where(is_key, gain_ref[...], F32(1))
        done = (raw * level * gain).astype(BF16)
        out_ref[...] = jnp.dot(hot_ref[...], done, preferred_element_type=F32).astype(BF16)


def project(table, hot, gain, rows, sib_rows, weights):
    across = pl.BlockSpec((LOC, RUN), lambda t, table: (0, table[t]))
    return pl.pallas_call(
        project_kernel,
        grid_spec=pltpu.PrefetchScalarGridSpec(
            num_scalar_prefetch=1,
            grid=(4,),
            in_specs=[
                whole((2 * SLOTS, PAIR)),
                whole((1, ROW_WIDTH)),
                across,
                across,
            ]
            + [pl.BlockSpec(memory_space=pl.ANY)] * 8,
            out_specs=whole((2 * SLOTS, ROW_WIDTH)),
            scratch_shapes=[
                pltpu.VMEM((WIDTH, ROW_WIDTH), BF16),
                pltpu.VMEM((PAIR, ROW_WIDTH), F32),
                pltpu.SemaphoreType.DMA((4, 4)),
            ],
        ),
        out_shape=jax.ShapeDtypeStruct((2 * SLOTS, ROW_WIDTH), BF16),
        compiler_params=pltpu.CompilerParams(**PARAMS),
        cost_estimate=pl.CostEstimate(
            flops=2 * PAIR * WIDTH * ROW_WIDTH, bytes_accessed=12 << 20, transcendentals=0
        ),
        name="project",
    )(table, hot, gain, rows, sib_rows, *weights)


def places_kernel(core_ref, own_ref, sib_ref, out_ref):
    for n, code in enumerate((own_ref, sib_ref)):
        k = core_ref[0] if n == 0 else 1 - core_ref[0]
        row = code[...].astype(F32).T[0:1].astype(jnp.int32) - 1
        out_ref[k] = onehot(iota((LOC, SLOTS), 0) == row)


def places(core, own_code, sib_code):
    return pl.pallas_call(
        places_kernel,
        in_specs=[pl.BlockSpec(memory_space=pltpu.SMEM)] + [pl.BlockSpec(memory_space=pltpu.VMEM)] * 2,
        out_shape=jax.ShapeDtypeStruct((2, LOC, SLOTS), BF16),
        compiler_params=pltpu.CompilerParams(**PARAMS),
        cost_estimate=pl.CostEstimate(flops=SLOTS * LOC * 8, bytes_accessed=1 << 20, transcendentals=0),
        name="places",
    )(core, own_code, sib_code)


def unpack_queries_kernel(core_ref, hot_ref, q_ref, out_ref):
    out_ref[...] = jnp.dot(hot_ref[core_ref[0]], q_ref[...], preferred_element_type=F32).astype(BF16)


def unpack_queries(core, hots, got, groups):
    return pl.pallas_call(
        unpack_queries_kernel,
        grid=(groups,),
        in_specs=[
            pl.BlockSpec(memory_space=pltpu.SMEM),
            whole((2, LOC, SLOTS)),
            pl.BlockSpec((SLOTS, GROUP_WIDTH), lambda i: (0, i)),
        ],
        out_specs=pl.BlockSpec((LOC, GROUP_WIDTH), lambda i: (0, i)),
        out_shape=jax.ShapeDtypeStruct((LOC, groups * GROUP_WIDTH), BF16),
        compiler_params=pltpu.CompilerParams(**PARAMS),
        cost_estimate=pl.CostEstimate(
            flops=2 * SLOTS * LOC * groups * GROUP_WIDTH, bytes_accessed=4 << 20, transcendentals=0
        ),
        name="unpack_queries",
    )(core, hots, got)


def unpack_kernel(hot_ref, seg_ref, got_ref, out_ref):
    got = got_ref[...].reshape(RANKS, 2, CAPACITY, ROW_WIDTH)
    for k in range(2):
        part = got[:, k].reshape(SLOTS, ROW_WIDTH)
        out_ref[k * LOC : (k + 1) * LOC, :] = jnp.dot(
            hot_ref[k], part, preferred_element_type=F32
        ).astype(BF16)
    seg = seg_ref[...].astype(F32).astype(BF16)
    for k in range(2):
        both = jnp.concatenate([seg[:, k * LOC : (k + 1) * LOC]] * 2, axis=1)
        out_ref[PAIR + 16 * k : PAIR + 16 * k + 16, :] = jnp.broadcast_to(both, (16, ROW_WIDTH))


def unpack(hots, seg, got):
    return pl.pallas_call(
        unpack_kernel,
        out_shape=jax.ShapeDtypeStruct((SENT, ROW_WIDTH), BF16),
        compiler_params=pltpu.CompilerParams(**PARAMS),
        cost_estimate=pl.CostEstimate(
            flops=2 * PAIR * SLOTS * ROW_WIDTH, bytes_accessed=3 << 20, transcendentals=0
        ),
        name="unpack",
    )(hots, seg, got)


def attend_kernel(
    packed, where_ref, seg_ref, hot_ref, q_ref, a0, a1, a2, b0, b1, b2, *rest
):
    out_ref, keys, values, bias, queries = rest[-5:]
    core = where_ref[0]
    ctx = where_ref[3]
    head = pl.program_id(0)

    @pl.when(head == 0)
    def _():
        @pl.when(core == 0)
        def _():
            for dst, (s0, s1, s2) in ((keys, (a0, a1, a2)), (values, (b0, b1, b2))):
                dst[0:PAIR, :] = s2[0:PAIR, :]
                dst[PAIR : 2 * PAIR, :] = s1[0:PAIR, :]
                dst[2 * PAIR : WINDOW, :] = s0[0:LOC, :]

        @pl.when(core != 0)
        def _():
            for dst, (s0, s1, s2) in ((keys, (b0, b1, b2)), (values, (a0, a1, a2))):
                dst[0:LOC, :] = s2[LOC:PAIR, :]
                dst[LOC : LOC + PAIR, :] = s1[0:PAIR, :]
                dst[LOC + PAIR : WINDOW, :] = s0[0:PAIR, :]

        segs = []
        for a in (a2, a1, a0):
            for start in (PAIR, PAIR + 16):
                segs.append(a[start : start + 16, :][0:1].astype(F32))
        left, right = jnp.concatenate(segs[:5], axis=1), jnp.concatenate(segs[1:], axis=1)
        key_seg = jnp.where(core == 0, left, right)
        query_seg = seg_ref[...].astype(F32)
        k = iota((LOC, WINDOW), 1)
        q = iota((LOC, WINDOW), 0)
        allowed = (k <= q + REACH) & (k >= REACH - ctx * LOC) & (key_seg == query_seg)
        bias[...] = jnp.where(allowed, F32(0), F32(-1e30))

    if packed:
        queries[...] = jnp.dot(hot_ref[core], q_ref[...], preferred_element_type=F32).astype(BF16)
    else:
        queries[...] = q_ref[...]
    columns = pl.ds(pl.multiple_of(head * HEAD_SIZE, HEAD_SIZE), HEAD_SIZE)
    key_rows = keys[:, columns]
    value_rows = values[:, columns]
    value_rows = jnp.concatenate([value_rows, jnp.ones_like(value_rows)], axis=1)
    for g in range(HEAD_GROUP):
        cols = slice(g * HEAD_SIZE, (g + 1) * HEAD_SIZE)
        scores = lax.dot_general(
            queries[:, cols], key_rows, (((1,), (1,)), ((), ())), preferred_element_type=F32
        )
        scores = scores + bias[...]
        best = jnp.max(scores, axis=-1, keepdims=True)
        p = jnp.exp2((scores - best) * SCORE_BASE2).astype(BF16)
        summed = jnp.dot(p, value_rows, preferred_element_type=F32)
        out_ref[:, cols] = (summed[:, :HEAD_SIZE] / summed[:, HEAD_SIZE:]).astype(BF16)


def attend(where, seg_col, hots, queries, part, mine, other, start):
    heads = KEY_VALUE_HEADS // 2
    packed = queries.shape[0] == SLOTS
    first = 0 if part * heads < EARLY else EARLY
    return pl.pallas_call(
        functools.partial(attend_kernel, packed),
        grid=(heads,),
        in_specs=[
            pl.BlockSpec(memory_space=pltpu.SMEM),
            whole((LOC, 1)),
            whole((2, LOC, SLOTS)),
            pl.BlockSpec((queries.shape[0], GROUP_WIDTH), lambda i: (0, part * heads - first + i)),
        ]
        + [pl.BlockSpec((SENT, HALF), lambda i: (0, part))] * 6
        + [pl.BlockSpec(memory_space=pl.ANY)] * len(start),
        out_specs=pl.BlockSpec((LOC, GROUP_WIDTH), lambda i: (0, part * heads + i)),
        out_shape=jax.ShapeDtypeStruct((LOC, QUERY_WIDTH), BF16),
        input_output_aliases={10: 0} if start else {},
        scratch_shapes=[
            pltpu.VMEM((WINDOW, HALF), BF16),
            pltpu.VMEM((WINDOW, HALF), BF16),
            pltpu.VMEM((LOC, WINDOW), F32),
            pltpu.VMEM((LOC, GROUP_WIDTH), BF16),
        ],
        compiler_params=pltpu.CompilerParams(**PARAMS),
        cost_estimate=pl.CostEstimate(
            flops=2 * LOC * WINDOW * QUERY_WIDTH,
            bytes_accessed=4 << 20,
            transcendentals=LOC * WINDOW * QUERY_HEADS // 2,
        ),
        name="attend",
    )(where, seg_col, hots, queries, *mine, *other, *start)


def chips():
    return [(x, y, z, k) for x in range(4) for z in range(8) for y in range(4) for k in range(2)]


def device(x, y, z, k):
    return (x % 4 * 8 + z % 8) * 8 + y % 4 * 2 + k


def shift(array, moved):
    pairs = [(device(*c), device(*moved(*c))) for c in chips()]
    return lax.ppermute(array, ("dp", "ctx"), pairs)


def swap_cores(array):
    return shift(array, lambda x, y, z, k: (x, y, z, 1 - k))


def send_up(array, by):
    pairs = [(device(*c), device(c[0], c[1] + by, c[2], c[3])) for c in chips() if c[1] + by < 4]
    return lax.ppermute(array, ("dp", "ctx"), pairs)


def along_z(array):
    groups = [[device(x, y, z, k) for z in range(8)] for x in range(4) for y in range(4) for k in range(2)]
    copies = jnp.broadcast_to(array[None], (8,) + array.shape)
    got = lax.all_to_all(copies, ("dp", "ctx"), 0, 0, axis_index_groups=groups, tiled=True)
    return got.reshape(8 * array.shape[0], array.shape[1])


def along_first(array, by):
    return shift(array, lambda x, y, z, k: (x + by, y, z, k) if k == 0 else (x, y + by, z, k))


def along_second(array, by):
    return shift(array, lambda x, y, z, k: (x, y + by, z, k) if k == 0 else (x + by, y, z, k))


def move(slots, rows):
    width = slots.shape[1]
    sent = slots.reshape(RANKS, rows, width)
    return lax.all_to_all(sent, "dp", split_axis=0, concat_axis=0, tiled=True).reshape(RANKS * rows, width)


def body(gen_rows, gen_queries, place, segment, key_value_weight, key_norm_gain):
    ctx = lax.axis_index("ctx")
    core, chip_y = ctx % 2, ctx // 2
    chip_x = lax.axis_index("dp") // 8
    where = jnp.stack([core, chip_x, chip_y, ctx])
    core_s = core.reshape(1)
    seg = segment.reshape(LOC)
    col, row = place.reshape(LOC, 1), place.reshape(1, LOC)

    part = lax.dynamic_slice_in_dim(
        key_value_weight, core * ROW_WIDTH + chip_y * HEAD_SIZE, HEAD_SIZE, 1
    )
    run = along_z(part)
    early_slots, late_slots = pack_queries(col, row, gen_queries)
    near = jnp.concatenate([run, along_first(run, 1)])
    far = jnp.concatenate([along_first(run, -1), along_first(run, 2)])
    early_slots, near, far = lax.optimization_barrier((early_slots, near, far))
    got_early = move(early_slots, CAPACITY)

    sib = swap_cores(jnp.stack([place, seg]))
    sib_rows = swap_cores(gen_rows)
    sib_col, sib_row = sib[0].reshape(LOC, 1), sib[0].reshape(1, LOC)
    pair_seg = jnp.where(core == 0, jnp.concatenate([seg, sib[1]]), jnp.concatenate([sib[1], seg]))
    pair_seg = pair_seg.reshape(1, PAIR)

    below, below_far = along_second(near, 1), along_second(far, 1)
    above, above_far = along_second(near, -1), along_second(far, -1)
    opposite, opposite_far = along_second(above, -1), along_second(below_far, 1)
    weights = [near, far, below, below_far, above, above_far, opposite, opposite_far]
    hot = row_places(core_s, col, row, sib_col, sib_row)
    offsets = jnp.array(NEAR)
    table = jnp.concatenate([(chip_x + offsets) % 4, (chip_y + offsets) % 4, core_s])
    slots = project(table, hot, key_norm_gain.reshape(1, ROW_WIDTH), gen_rows, sib_rows, weights)
    slots, got_early = lax.optimization_barrier((slots, got_early))
    got = move(slots, 2 * CAPACITY)
    own_code = got_early[:, EARLY * GROUP_WIDTH :]
    hots = places(core_s, own_code, swap_cores(own_code))
    early = unpack_queries(core_s, hots, got_early, EARLY)
    got, early, hots = lax.optimization_barrier((got, early, hots))
    own = unpack(hots, pair_seg, got)
    late_slots, own = lax.optimization_barrier((late_slots, own))
    up = [send_up(own, 1), send_up(own, 2)]
    got_late = move(late_slots, CAPACITY)
    other = [swap_cores(m) for m in [own] + up]
    seg_col = seg.reshape(LOC, 1)
    mine = [own] + up
    out = attend(where, seg_col, hots, early, 0, mine, other, [])
    got_late, out = lax.optimization_barrier((got_late, out))
    return attend(where, seg_col, hots, got_late, 1, mine, other, [out])


def solution(mesh):
    placed = (
        P(("dp", "ctx"), None),
        P(("dp", "ctx"), None),
        P(("dp", "ctx")),
        P("dp", "ctx"),
        P("dp", None),
        P(),
    )
    return jax.shard_map(
        body, mesh=mesh, in_specs=placed, out_specs=P(("dp", "ctx"), None), check_vma=False
    )
```

```python
import functools

import jax
import jax.numpy as jnp
from jax import lax
from jax.experimental import pallas as pl
from jax.experimental.pallas import tpu as pltpu
from jax.sharding import PartitionSpec as P

LOC = 256
RANKS = 32
CAPACITY = 16
SLOTS = RANKS * CAPACITY
WIDTH = 5120
HEAD_SIZE = 128
QUERY_HEADS = 20
KEY_VALUE_HEADS = 4
HEAD_GROUP = QUERY_HEADS // KEY_VALUE_HEADS
ROW_WIDTH = KEY_VALUE_HEADS * HEAD_SIZE
QUERY_WIDTH = QUERY_HEADS * HEAD_SIZE
RANK_POSITIONS = 2048
PAIR = 2 * LOC
REACH = 1024
CODE_WIDTH = 128
NEAR = (0, -1, 1, -2)
RUN = WIDTH // 4
GROUP_WIDTH = HEAD_GROUP * HEAD_SIZE
EARLY = 2
WINDOW = REACH + LOC
SENT = PAIR + 32
HALF = ROW_WIDTH // 2
SCORE_BASE2 = 1.4426950408889634 * HEAD_SIZE ** (-0.5)
BF16 = jnp.bfloat16
F32 = jnp.float32
PARAMS = dict(vmem_limit_bytes=24 << 20)


def whole(shape):
    return pl.BlockSpec(shape, lambda *_: (0,) * len(shape))


def iota(shape, dim):
    return lax.broadcasted_iota(jnp.int32, shape, dim)


def order_rows(col, row):
    same = (col // RANK_POSITIONS) == (row // RANK_POSITIONS)
    earlier = iota((LOC, LOC), 0) < iota((LOC, LOC), 1)
    order = jnp.sum((same & earlier).astype(jnp.int32), axis=0, keepdims=True)
    return row // RANK_POSITIONS, order


def order_cols(col, row):
    same = (col // RANK_POSITIONS) == (row // RANK_POSITIONS)
    earlier = iota((LOC, LOC), 1) < iota((LOC, LOC), 0)
    order = jnp.sum((same & earlier).astype(jnp.int32), axis=1, keepdims=True)
    return col // RANK_POSITIONS, order


def onehot(mask):
    return jnp.where(mask, F32(1), F32(0)).astype(BF16)


def pick(mask, values):
    return jnp.dot(onehot(mask), values, preferred_element_type=F32).astype(BF16)


def pack_queries_kernel(col_ref, row_ref, q_ref, early_ref, late_ref, hot):
    step = pl.program_id(0)

    @pl.when(step == 0)
    def _():
        target, order = order_rows(col_ref[...], row_ref[...])
        hot[...] = onehot(iota((SLOTS, LOC), 0) == target * CAPACITY + order)
        code = jnp.broadcast_to(col_ref[...] % LOC + 1, (LOC, CODE_WIDTH)).astype(F32).astype(BF16)
        early_ref[:, EARLY * GROUP_WIDTH :] = jnp.dot(
            hot[...], code, preferred_element_type=F32
        ).astype(BF16)

    packed = jnp.dot(hot[...], q_ref[...], preferred_element_type=F32).astype(BF16)
    for group in range(KEY_VALUE_HEADS):
        ref, first = (early_ref, 0) if group < EARLY else (late_ref, EARLY)

        @pl.when(step == group)
        def _(ref=ref, first=first, group=group):
            ref[:, (group - first) * GROUP_WIDTH : (group - first + 1) * GROUP_WIDTH] = packed


def pack_queries(col, row, queries):
    widths = (EARLY * GROUP_WIDTH + CODE_WIDTH, (KEY_VALUE_HEADS - EARLY) * GROUP_WIDTH)
    return pl.pallas_call(
        pack_queries_kernel,
        grid=(KEY_VALUE_HEADS,),
        in_specs=[
            whole((LOC, 1)),
            whole((1, LOC)),
            pl.BlockSpec((LOC, GROUP_WIDTH), lambda i: (0, i)),
        ],
        out_specs=[whole((SLOTS, w)) for w in widths],
        out_shape=[jax.ShapeDtypeStruct((SLOTS, w), BF16) for w in widths],
        scratch_shapes=[pltpu.VMEM((SLOTS, LOC), BF16)],
        compiler_params=pltpu.CompilerParams(**PARAMS),
        cost_estimate=pl.CostEstimate(
            flops=2 * SLOTS * LOC * QUERY_WIDTH, bytes_accessed=4 << 20, transcendentals=0
        ),
        name="pack_queries",
    )(col, row, queries)


def row_places_kernel(core_ref, col_ref, row_ref, sib_col_ref, sib_row_ref, out_ref):
    core = core_ref[0]
    for n, (col, row, k) in enumerate(((col_ref, row_ref, core), (sib_col_ref, sib_row_ref, 1 - core))):
        target, order = order_rows(col[...], row[...])
        slot = target * (2 * CAPACITY) + k * CAPACITY + order
        out_ref[:, n * LOC : (n + 1) * LOC] = onehot(iota((2 * SLOTS, LOC), 0) == slot)


def row_places(core, col, row, sib_col, sib_row):
    return pl.pallas_call(
        row_places_kernel,
        in_specs=[pl.BlockSpec(memory_space=pltpu.SMEM)] + [pl.BlockSpec(memory_space=pltpu.VMEM)] * 4,
        out_shape=jax.ShapeDtypeStruct((2 * SLOTS, PAIR), BF16),
        compiler_params=pltpu.CompilerParams(**PARAMS),
        cost_estimate=pl.CostEstimate(
            flops=2 * SLOTS * PAIR * 8, bytes_accessed=1 << 20, transcendentals=0
        ),
        name="row_places",
    )(core, col, row, sib_col, sib_row)


def project_kernel(
    table_ref, hot_ref, gain_ref, x_ref, sib_ref, *rest
):
    step = pl.program_id(0)
    core = table_ref[8]
    sources, (out_ref, weight, acc, sems) = rest[:8], rest[8:]

    def copy(j, i, x, y):
        return pltpu.make_async_copy(
            sources[2 * j + i // 2].at[pl.ds(i % 2 * RUN, RUN), :],
            weight.at[
                pl.ds(pl.multiple_of(x * RUN, RUN), RUN),
                pl.ds(pl.multiple_of(y * HEAD_SIZE, HEAD_SIZE), HEAD_SIZE),
            ],
            sems.at[x, y],
        )

    @pl.when(step == 0)
    def _():
        @pl.when(core == 0)
        def _():
            for i in range(4):
                for j in range(4):
                    copy(j, i, table_ref[i], table_ref[4 + j]).start()

        @pl.when(core != 0)
        def _():
            for j in range(4):
                for i in range(4):
                    copy(j, i, table_ref[j], table_ref[4 + i]).start()

    x = table_ref[step]
    for y in range(4):
        copy(0, 0, x, y).wait()
    w = weight[pl.ds(pl.multiple_of(x * RUN, RUN), RUN), :]
    for n, ref in enumerate((x_ref, sib_ref)):
        now = jnp.dot(ref[...], w, preferred_element_type=F32)
        part = slice(n * LOC, (n + 1) * LOC)

        @pl.when(step == 0)
        def _(now=now, part=part):
            acc[part, :] = now

        @pl.when(step > 0)
        def _(now=now, part=part):
            acc[part, :] += now

    @pl.when(step == 3)
    def _():
        is_key = core == 0
        raw = acc[...]
        level = lax.rsqrt(jnp.mean(raw * raw, axis=-1, keepdims=True) + 1e-06)
        level = jnp.where(is_key, level, F32(1))
        gain = jnp.where(is_key, gain_ref[...], F32(1))
        done = (raw * level * gain).astype(BF16)
        out_ref[...] = jnp.dot(hot_ref[...], done, preferred_element_type=F32).astype(BF16)


def project(table, hot, gain, rows, sib_rows, weights):
    across = pl.BlockSpec((LOC, RUN), lambda t, table: (0, table[t]))
    return pl.pallas_call(
        project_kernel,
        grid_spec=pltpu.PrefetchScalarGridSpec(
            num_scalar_prefetch=1,
            grid=(4,),
            in_specs=[
                whole((2 * SLOTS, PAIR)),
                whole((1, ROW_WIDTH)),
                across,
                across,
            ]
            + [pl.BlockSpec(memory_space=pl.ANY)] * 8,
            out_specs=whole((2 * SLOTS, ROW_WIDTH)),
            scratch_shapes=[
                pltpu.VMEM((WIDTH, ROW_WIDTH), BF16),
                pltpu.VMEM((PAIR, ROW_WIDTH), F32),
                pltpu.SemaphoreType.DMA((4, 4)),
            ],
        ),
        out_shape=jax.ShapeDtypeStruct((2 * SLOTS, ROW_WIDTH), BF16),
        compiler_params=pltpu.CompilerParams(**PARAMS),
        cost_estimate=pl.CostEstimate(
            flops=2 * PAIR * WIDTH * ROW_WIDTH, bytes_accessed=12 << 20, transcendentals=0
        ),
        name="project",
    )(table, hot, gain, rows, sib_rows, *weights)


def places_kernel(core_ref, own_ref, sib_ref, out_ref):
    for n, code in enumerate((own_ref, sib_ref)):
        k = core_ref[0] if n == 0 else 1 - core_ref[0]
        row = code[...].astype(F32).T[0:1].astype(jnp.int32) - 1
        out_ref[k] = onehot(iota((LOC, SLOTS), 0) == row)


def places(core, own_code, sib_code):
    return pl.pallas_call(
        places_kernel,
        in_specs=[pl.BlockSpec(memory_space=pltpu.SMEM)] + [pl.BlockSpec(memory_space=pltpu.VMEM)] * 2,
        out_shape=jax.ShapeDtypeStruct((2, LOC, SLOTS), BF16),
        compiler_params=pltpu.CompilerParams(**PARAMS),
        cost_estimate=pl.CostEstimate(flops=SLOTS * LOC * 8, bytes_accessed=1 << 20, transcendentals=0),
        name="places",
    )(core, own_code, sib_code)


def unpack_queries_kernel(core_ref, hot_ref, q_ref, out_ref):
    out_ref[...] = jnp.dot(hot_ref[core_ref[0]], q_ref[...], preferred_element_type=F32).astype(BF16)


def unpack_queries(core, hots, got, groups):
    return pl.pallas_call(
        unpack_queries_kernel,
        grid=(groups,),
        in_specs=[
            pl.BlockSpec(memory_space=pltpu.SMEM),
            whole((2, LOC, SLOTS)),
            pl.BlockSpec((SLOTS, GROUP_WIDTH), lambda i: (0, i)),
        ],
        out_specs=pl.BlockSpec((LOC, GROUP_WIDTH), lambda i: (0, i)),
        out_shape=jax.ShapeDtypeStruct((LOC, groups * GROUP_WIDTH), BF16),
        compiler_params=pltpu.CompilerParams(**PARAMS),
        cost_estimate=pl.CostEstimate(
            flops=2 * SLOTS * LOC * groups * GROUP_WIDTH, bytes_accessed=4 << 20, transcendentals=0
        ),
        name="unpack_queries",
    )(core, hots, got)


def unpack_kernel(hot_ref, seg_ref, got_ref, out_ref):
    got = got_ref[...].reshape(RANKS, 2, CAPACITY, ROW_WIDTH)
    for k in range(2):
        part = got[:, k].reshape(SLOTS, ROW_WIDTH)
        out_ref[k * LOC : (k + 1) * LOC, :] = jnp.dot(
            hot_ref[k], part, preferred_element_type=F32
        ).astype(BF16)
    seg = seg_ref[...].astype(F32).astype(BF16)
    for k in range(2):
        both = jnp.concatenate([seg[:, k * LOC : (k + 1) * LOC]] * 2, axis=1)
        out_ref[PAIR + 16 * k : PAIR + 16 * k + 16, :] = jnp.broadcast_to(both, (16, ROW_WIDTH))


def unpack(hots, seg, got):
    return pl.pallas_call(
        unpack_kernel,
        out_shape=jax.ShapeDtypeStruct((SENT, ROW_WIDTH), BF16),
        compiler_params=pltpu.CompilerParams(**PARAMS),
        cost_estimate=pl.CostEstimate(
            flops=2 * PAIR * SLOTS * ROW_WIDTH, bytes_accessed=3 << 20, transcendentals=0
        ),
        name="unpack",
    )(hots, seg, got)


def attend_kernel(
    packed, where_ref, seg_ref, hot_ref, q_ref, a0, a1, a2, b0, b1, b2, *rest
):
    out_ref, keys, values, bias, queries = rest[-5:]
    core = where_ref[0]
    ctx = where_ref[3]
    head = pl.program_id(0)

    @pl.when(head == 0)
    def _():
        @pl.when(core == 0)
        def _():
            for dst, (s0, s1, s2) in ((keys, (a0, a1, a2)), (values, (b0, b1, b2))):
                dst[0:PAIR, :] = s2[0:PAIR, :]
                dst[PAIR : 2 * PAIR, :] = s1[0:PAIR, :]
                dst[2 * PAIR : WINDOW, :] = s0[0:LOC, :]

        @pl.when(core != 0)
        def _():
            for dst, (s0, s1, s2) in ((keys, (b0, b1, b2)), (values, (a0, a1, a2))):
                dst[0:LOC, :] = s2[LOC:PAIR, :]
                dst[LOC : LOC + PAIR, :] = s1[0:PAIR, :]
                dst[LOC + PAIR : WINDOW, :] = s0[0:PAIR, :]

        segs = []
        for a in (a2, a1, a0):
            for start in (PAIR, PAIR + 16):
                segs.append(a[start : start + 16, :][0:1].astype(F32))
        left, right = jnp.concatenate(segs[:5], axis=1), jnp.concatenate(segs[1:], axis=1)
        key_seg = jnp.where(core == 0, left, right)
        query_seg = seg_ref[...].astype(F32)
        k = iota((LOC, WINDOW), 1)
        q = iota((LOC, WINDOW), 0)
        allowed = (k <= q + REACH) & (k >= REACH - ctx * LOC) & (key_seg == query_seg)
        bias[...] = jnp.where(allowed, F32(0), F32(-1e30))

    if packed:
        queries[...] = jnp.dot(hot_ref[core], q_ref[...], preferred_element_type=F32).astype(BF16)
    else:
        queries[...] = q_ref[...]
    columns = pl.ds(pl.multiple_of(head * HEAD_SIZE, HEAD_SIZE), HEAD_SIZE)
    key_rows = keys[:, columns]
    value_rows = values[:, columns]
    value_rows = jnp.concatenate([value_rows, jnp.ones_like(value_rows)], axis=1)
    for g in range(HEAD_GROUP):
        cols = slice(g * HEAD_SIZE, (g + 1) * HEAD_SIZE)
        scores = lax.dot_general(
            queries[:, cols], key_rows, (((1,), (1,)), ((), ())), preferred_element_type=F32
        )
        scores = scores + bias[...]
        best = jnp.max(scores, axis=-1, keepdims=True)
        p = jnp.exp2((scores - best) * SCORE_BASE2).astype(BF16)
        summed = jnp.dot(p, value_rows, preferred_element_type=F32)
        out_ref[:, cols] = (summed[:, :HEAD_SIZE] / summed[:, HEAD_SIZE:]).astype(BF16)


def attend(where, seg_col, hots, queries, part, mine, other, start):
    heads = KEY_VALUE_HEADS // 2
    packed = queries.shape[0] == SLOTS
    first = 0 if part * heads < EARLY else EARLY
    return pl.pallas_call(
        functools.partial(attend_kernel, packed),
        grid=(heads,),
        in_specs=[
            pl.BlockSpec(memory_space=pltpu.SMEM),
            whole((LOC, 1)),
            whole((2, LOC, SLOTS)),
            pl.BlockSpec((queries.shape[0], GROUP_WIDTH), lambda i: (0, part * heads - first + i)),
        ]
        + [pl.BlockSpec((SENT, HALF), lambda i: (0, part))] * 6
        + [pl.BlockSpec(memory_space=pl.ANY)] * len(start),
        out_specs=pl.BlockSpec((LOC, GROUP_WIDTH), lambda i: (0, part * heads + i)),
        out_shape=jax.ShapeDtypeStruct((LOC, QUERY_WIDTH), BF16),
        input_output_aliases={10: 0} if start else {},
        scratch_shapes=[
            pltpu.VMEM((WINDOW, HALF), BF16),
            pltpu.VMEM((WINDOW, HALF), BF16),
            pltpu.VMEM((LOC, WINDOW), F32),
            pltpu.VMEM((LOC, GROUP_WIDTH), BF16),
        ],
        compiler_params=pltpu.CompilerParams(**PARAMS),
        cost_estimate=pl.CostEstimate(
            flops=2 * LOC * WINDOW * QUERY_WIDTH,
            bytes_accessed=4 << 20,
            transcendentals=LOC * WINDOW * QUERY_HEADS // 2,
        ),
        name="attend",
    )(where, seg_col, hots, queries, *mine, *other, *start)


def chips():
    return [(x, y, z, k) for x in range(4) for z in range(8) for y in range(4) for k in range(2)]


def device(x, y, z, k):
    return (x % 4 * 8 + z % 8) * 8 + y % 4 * 2 + k


def shift(array, moved):
    pairs = [(device(*c), device(*moved(*c))) for c in chips()]
    return lax.ppermute(array, ("dp", "ctx"), pairs)


def swap_cores(array):
    return shift(array, lambda x, y, z, k: (x, y, z, 1 - k))


def send_up(array, by):
    pairs = [(device(*c), device(c[0], c[1] + by, c[2], c[3])) for c in chips() if c[1] + by < 4]
    return lax.ppermute(array, ("dp", "ctx"), pairs)


def along_z(array):
    groups = [[device(x, y, z, k) for z in range(8)] for x in range(4) for y in range(4) for k in range(2)]
    copies = jnp.broadcast_to(array[None], (8,) + array.shape)
    got = lax.all_to_all(copies, ("dp", "ctx"), 0, 0, axis_index_groups=groups, tiled=True)
    return got.reshape(8 * array.shape[0], array.shape[1])


def along_first(array, by):
    return shift(array, lambda x, y, z, k: (x + by, y, z, k) if k == 0 else (x, y + by, z, k))


def along_second(array, by):
    return shift(array, lambda x, y, z, k: (x, y + by, z, k) if k == 0 else (x + by, y, z, k))


def move(slots, rows):
    width = slots.shape[1]
    sent = slots.reshape(RANKS, rows, width)
    return lax.all_to_all(sent, "dp", split_axis=0, concat_axis=0, tiled=True).reshape(RANKS * rows, width)


def body(gen_rows, gen_queries, place, segment, key_value_weight, key_norm_gain):
    ctx = lax.axis_index("ctx")
    core, chip_y = ctx % 2, ctx // 2
    chip_x = lax.axis_index("dp") // 8
    where = jnp.stack([core, chip_x, chip_y, ctx])
    core_s = core.reshape(1)
    seg = segment.reshape(LOC)
    col, row = place.reshape(LOC, 1), place.reshape(1, LOC)

    part = lax.dynamic_slice_in_dim(
        key_value_weight, core * ROW_WIDTH + chip_y * HEAD_SIZE, HEAD_SIZE, 1
    )
    run = along_z(part)
    (early_slots, late_slots), run = lax.optimization_barrier((pack_queries(col, row, gen_queries), run))
    near = jnp.concatenate([run, along_first(run, 1)])
    far = jnp.concatenate([along_first(run, -1), along_first(run, 2)])
    early_slots, near, far = lax.optimization_barrier((early_slots, near, far))
    got_early = move(early_slots, CAPACITY)

    sib = swap_cores(jnp.stack([place, seg]))
    sib_rows = swap_cores(gen_rows)
    sib_col, sib_row = sib[0].reshape(LOC, 1), sib[0].reshape(1, LOC)
    pair_seg = jnp.where(core == 0, jnp.concatenate([seg, sib[1]]), jnp.concatenate([sib[1], seg]))
    pair_seg = pair_seg.reshape(1, PAIR)

    below, below_far = along_second(near, 1), along_second(far, 1)
    above, above_far = along_second(near, -1), along_second(far, -1)
    opposite, opposite_far = along_second(above, -1), along_second(below_far, 1)
    weights = [near, far, below, below_far, above, above_far, opposite, opposite_far]
    hot = row_places(core_s, col, row, sib_col, sib_row)
    offsets = jnp.array(NEAR)
    table = jnp.concatenate([(chip_x + offsets) % 4, (chip_y + offsets) % 4, core_s])
    slots = project(table, hot, key_norm_gain.reshape(1, ROW_WIDTH), gen_rows, sib_rows, weights)
    slots, got_early = lax.optimization_barrier((slots, got_early))
    got = move(slots, 2 * CAPACITY)
    own_code = got_early[:, EARLY * GROUP_WIDTH :]
    hots = places(core_s, own_code, swap_cores(own_code))
    early = unpack_queries(core_s, hots, got_early, EARLY)
    got, early, hots = lax.optimization_barrier((got, early, hots))
    own = unpack(hots, pair_seg, got)
    late_slots, own = lax.optimization_barrier((late_slots, own))
    up = [send_up(own, 1), send_up(own, 2)]
    got_late = move(late_slots, CAPACITY)
    other = [swap_cores(m) for m in [own] + up]
    seg_col = seg.reshape(LOC, 1)
    mine = [own] + up
    out = attend(where, seg_col, hots, early, 0, mine, other, [])
    got_late, out = lax.optimization_barrier((got_late, out))
    return attend(where, seg_col, hots, got_late, 1, mine, other, [out])


def solution(mesh):
    placed = (
        P(("dp", "ctx"), None),
        P(("dp", "ctx"), None),
        P(("dp", "ctx")),
        P("dp", "ctx"),
        P("dp", None),
        P(),
    )
    return jax.shard_map(
        body, mesh=mesh, in_specs=placed, out_specs=P(("dp", "ctx"), None), check_vma=False
    )
```

```python
import functools

import jax
import jax.numpy as jnp
from jax import lax
from jax.experimental import pallas as pl
from jax.experimental.pallas import tpu as pltpu
from jax.sharding import PartitionSpec as P

LOC = 256
RANKS = 32
CAPACITY = 16
SLOTS = RANKS * CAPACITY
WIDTH = 5120
HEAD_SIZE = 128
QUERY_HEADS = 20
KEY_VALUE_HEADS = 4
HEAD_GROUP = QUERY_HEADS // KEY_VALUE_HEADS
ROW_WIDTH = KEY_VALUE_HEADS * HEAD_SIZE
QUERY_WIDTH = QUERY_HEADS * HEAD_SIZE
RANK_POSITIONS = 2048
PAIR = 2 * LOC
REACH = 1024
CODE_WIDTH = 128
NEAR = (0, -1, 1, -2)
RUN = WIDTH // 4
GROUP_WIDTH = HEAD_GROUP * HEAD_SIZE
EARLY = 2
WINDOW = REACH + LOC
SENT = PAIR + 32
HALF = ROW_WIDTH // 2
SCORE_BASE2 = 1.4426950408889634 * HEAD_SIZE ** (-0.5)
BF16 = jnp.bfloat16
F32 = jnp.float32
PARAMS = dict(vmem_limit_bytes=24 << 20)


def whole(shape):
    return pl.BlockSpec(shape, lambda *_: (0,) * len(shape))


def iota(shape, dim):
    return lax.broadcasted_iota(jnp.int32, shape, dim)


def order_rows(col, row):
    same = (col // RANK_POSITIONS) == (row // RANK_POSITIONS)
    earlier = iota((LOC, LOC), 0) < iota((LOC, LOC), 1)
    order = jnp.sum((same & earlier).astype(jnp.int32), axis=0, keepdims=True)
    return row // RANK_POSITIONS, order


def order_cols(col, row):
    same = (col // RANK_POSITIONS) == (row // RANK_POSITIONS)
    earlier = iota((LOC, LOC), 1) < iota((LOC, LOC), 0)
    order = jnp.sum((same & earlier).astype(jnp.int32), axis=1, keepdims=True)
    return col // RANK_POSITIONS, order


def onehot(mask):
    return jnp.where(mask, F32(1), F32(0)).astype(BF16)


def pick(mask, values):
    return jnp.dot(onehot(mask), values, preferred_element_type=F32).astype(BF16)


def pack_queries_kernel(col_ref, row_ref, q_ref, early_ref, late_ref, hot):
    step = pl.program_id(0)

    @pl.when(step == 0)
    def _():
        target, order = order_rows(col_ref[...], row_ref[...])
        hot[...] = onehot(iota((SLOTS, LOC), 0) == target * CAPACITY + order)
        code = jnp.broadcast_to(col_ref[...] % LOC + 1, (LOC, CODE_WIDTH)).astype(F32).astype(BF16)
        early_ref[:, EARLY * GROUP_WIDTH :] = jnp.dot(
            hot[...], code, preferred_element_type=F32
        ).astype(BF16)

    packed = jnp.dot(hot[...], q_ref[...], preferred_element_type=F32).astype(BF16)
    for group in range(KEY_VALUE_HEADS):
        ref, first = (early_ref, 0) if group < EARLY else (late_ref, EARLY)

        @pl.when(step == group)
        def _(ref=ref, first=first, group=group):
            ref[:, (group - first) * GROUP_WIDTH : (group - first + 1) * GROUP_WIDTH] = packed


def pack_queries(col, row, queries):
    widths = (EARLY * GROUP_WIDTH + CODE_WIDTH, (KEY_VALUE_HEADS - EARLY) * GROUP_WIDTH)
    return pl.pallas_call(
        pack_queries_kernel,
        grid=(KEY_VALUE_HEADS,),
        in_specs=[
            whole((LOC, 1)),
            whole((1, LOC)),
            pl.BlockSpec((LOC, GROUP_WIDTH), lambda i: (0, i)),
        ],
        out_specs=[whole((SLOTS, w)) for w in widths],
        out_shape=[jax.ShapeDtypeStruct((SLOTS, w), BF16) for w in widths],
        scratch_shapes=[pltpu.VMEM((SLOTS, LOC), BF16)],
        compiler_params=pltpu.CompilerParams(**PARAMS),
        cost_estimate=pl.CostEstimate(
            flops=2 * SLOTS * LOC * QUERY_WIDTH, bytes_accessed=4 << 20, transcendentals=0
        ),
        name="pack_queries",
    )(col, row, queries)


def row_places_kernel(core_ref, col_ref, row_ref, sib_col_ref, sib_row_ref, out_ref):
    core = core_ref[0]
    for n, (col, row, k) in enumerate(((col_ref, row_ref, core), (sib_col_ref, sib_row_ref, 1 - core))):
        target, order = order_rows(col[...], row[...])
        slot = target * (2 * CAPACITY) + k * CAPACITY + order
        out_ref[:, n * LOC : (n + 1) * LOC] = onehot(iota((2 * SLOTS, LOC), 0) == slot)


def row_places(core, col, row, sib_col, sib_row):
    return pl.pallas_call(
        row_places_kernel,
        in_specs=[pl.BlockSpec(memory_space=pltpu.SMEM)] + [pl.BlockSpec(memory_space=pltpu.VMEM)] * 4,
        out_shape=jax.ShapeDtypeStruct((2 * SLOTS, PAIR), BF16),
        compiler_params=pltpu.CompilerParams(**PARAMS),
        cost_estimate=pl.CostEstimate(
            flops=2 * SLOTS * PAIR * 8, bytes_accessed=1 << 20, transcendentals=0
        ),
        name="row_places",
    )(core, col, row, sib_col, sib_row)


def project_kernel(table_ref, hot_ref, gain_ref, x_ref, sib_ref, *rest):
    sources, (out_ref, acc, done) = rest[:8], rest[8:]
    step = pl.program_id(0)
    core = table_ref[8]

    def add(blocks):
        w = jnp.concatenate(blocks, axis=1)
        x = jnp.concatenate([x_ref[...], sib_ref[...]], axis=0)
        acc[...] += jnp.dot(x, w, preferred_element_type=F32)

    @pl.when(step == 0)
    def _():
        acc[...] = jnp.zeros_like(acc)

    for t in range(4):

        @pl.when((step == t) & (core == 0))
        def _(t=t):
            rows = slice(t % 2 * RUN, (t % 2 + 1) * RUN)
            add([sources[2 * j + t // 2][rows, :] for j in range(4)])

        @pl.when((step == t) & (core != 0))
        def _(t=t):
            add([sources[2 * t + i // 2][i % 2 * RUN : (i % 2 + 1) * RUN, :] for i in range(4)])

    @pl.when(step == 3)
    def _():
        is_key = core == 0
        raw = acc[...]
        level = lax.rsqrt(jnp.mean(raw * raw, axis=-1, keepdims=True) + 1e-06)
        level = jnp.where(is_key, level, F32(1))
        for n in range(4):
            column = pl.ds(pl.multiple_of(table_ref[4 + n] * HEAD_SIZE, HEAD_SIZE), HEAD_SIZE)
            gain = jnp.where(is_key, gain_ref[:, column], F32(1))
            done[:, column] = (raw[:, n * HEAD_SIZE : (n + 1) * HEAD_SIZE] * level * gain).astype(BF16)
        out_ref[...] = jnp.dot(hot_ref[...], done[...], preferred_element_type=F32).astype(BF16)


def project(table, hot, gain, rows, sib_rows, weights):
    across = pl.BlockSpec((LOC, RUN), lambda t, table: (0, table[t]))
    return pl.pallas_call(
        project_kernel,
        grid_spec=pltpu.PrefetchScalarGridSpec(
            num_scalar_prefetch=1,
            grid=(4,),
            in_specs=[
                whole((2 * SLOTS, PAIR)),
                whole((1, ROW_WIDTH)),
                across,
                across,
            ]
            + [pl.BlockSpec(memory_space=pltpu.VMEM)] * 8,
            out_specs=whole((2 * SLOTS, ROW_WIDTH)),
            scratch_shapes=[pltpu.VMEM((PAIR, ROW_WIDTH), F32), pltpu.VMEM((PAIR, ROW_WIDTH), BF16)],
        ),
        out_shape=jax.ShapeDtypeStruct((2 * SLOTS, ROW_WIDTH), BF16),
        compiler_params=pltpu.CompilerParams(**PARAMS),
        cost_estimate=pl.CostEstimate(
            flops=2 * PAIR * WIDTH * ROW_WIDTH, bytes_accessed=12 << 20, transcendentals=0
        ),
        name="project",
    )(table, hot, gain, rows, sib_rows, *weights)


def places_kernel(core_ref, own_ref, sib_ref, out_ref):
    for n, code in enumerate((own_ref, sib_ref)):
        k = core_ref[0] if n == 0 else 1 - core_ref[0]
        row = code[...].astype(F32).T[0:1].astype(jnp.int32) - 1
        out_ref[k] = onehot(iota((LOC, SLOTS), 0) == row)


def places(core, own_code, sib_code):
    return pl.pallas_call(
        places_kernel,
        in_specs=[pl.BlockSpec(memory_space=pltpu.SMEM)] + [pl.BlockSpec(memory_space=pltpu.VMEM)] * 2,
        out_shape=jax.ShapeDtypeStruct((2, LOC, SLOTS), BF16),
        compiler_params=pltpu.CompilerParams(**PARAMS),
        cost_estimate=pl.CostEstimate(flops=SLOTS * LOC * 8, bytes_accessed=1 << 20, transcendentals=0),
        name="places",
    )(core, own_code, sib_code)


def unpack_queries_kernel(core_ref, hot_ref, q_ref, out_ref):
    out_ref[...] = jnp.dot(hot_ref[core_ref[0]], q_ref[...], preferred_element_type=F32).astype(BF16)


def unpack_queries(core, hots, got, groups):
    return pl.pallas_call(
        unpack_queries_kernel,
        grid=(groups,),
        in_specs=[
            pl.BlockSpec(memory_space=pltpu.SMEM),
            whole((2, LOC, SLOTS)),
            pl.BlockSpec((SLOTS, GROUP_WIDTH), lambda i: (0, i)),
        ],
        out_specs=pl.BlockSpec((LOC, GROUP_WIDTH), lambda i: (0, i)),
        out_shape=jax.ShapeDtypeStruct((LOC, groups * GROUP_WIDTH), BF16),
        compiler_params=pltpu.CompilerParams(**PARAMS),
        cost_estimate=pl.CostEstimate(
            flops=2 * SLOTS * LOC * groups * GROUP_WIDTH, bytes_accessed=4 << 20, transcendentals=0
        ),
        name="unpack_queries",
    )(core, hots, got)


def unpack_kernel(hot_ref, seg_ref, got_ref, out_ref):
    got = got_ref[...].reshape(RANKS, 2, CAPACITY, ROW_WIDTH)
    for k in range(2):
        part = got[:, k].reshape(SLOTS, ROW_WIDTH)
        out_ref[k * LOC : (k + 1) * LOC, :] = jnp.dot(
            hot_ref[k], part, preferred_element_type=F32
        ).astype(BF16)
    seg = seg_ref[...].astype(F32).astype(BF16)
    for k in range(2):
        both = jnp.concatenate([seg[:, k * LOC : (k + 1) * LOC]] * 2, axis=1)
        out_ref[PAIR + 16 * k : PAIR + 16 * k + 16, :] = jnp.broadcast_to(both, (16, ROW_WIDTH))


def unpack(hots, seg, got):
    return pl.pallas_call(
        unpack_kernel,
        out_shape=jax.ShapeDtypeStruct((SENT, ROW_WIDTH), BF16),
        compiler_params=pltpu.CompilerParams(**PARAMS),
        cost_estimate=pl.CostEstimate(
            flops=2 * PAIR * SLOTS * ROW_WIDTH, bytes_accessed=3 << 20, transcendentals=0
        ),
        name="unpack",
    )(hots, seg, got)


def attend_kernel(
    packed, where_ref, seg_ref, hot_ref, q_ref, a0, a1, a2, b0, b1, b2, *rest
):
    out_ref, keys, values, bias, queries = rest[-5:]
    core = where_ref[0]
    ctx = where_ref[3]
    head = pl.program_id(0)

    @pl.when(head == 0)
    def _():
        @pl.when(core == 0)
        def _():
            for dst, (s0, s1, s2) in ((keys, (a0, a1, a2)), (values, (b0, b1, b2))):
                dst[0:PAIR, :] = s2[0:PAIR, :]
                dst[PAIR : 2 * PAIR, :] = s1[0:PAIR, :]
                dst[2 * PAIR : WINDOW, :] = s0[0:LOC, :]

        @pl.when(core != 0)
        def _():
            for dst, (s0, s1, s2) in ((keys, (b0, b1, b2)), (values, (a0, a1, a2))):
                dst[0:LOC, :] = s2[LOC:PAIR, :]
                dst[LOC : LOC + PAIR, :] = s1[0:PAIR, :]
                dst[LOC + PAIR : WINDOW, :] = s0[0:PAIR, :]

        segs = []
        for a in (a2, a1, a0):
            for start in (PAIR, PAIR + 16):
                segs.append(a[start : start + 16, :][0:1].astype(F32))
        left, right = jnp.concatenate(segs[:5], axis=1), jnp.concatenate(segs[1:], axis=1)
        key_seg = jnp.where(core == 0, left, right)
        query_seg = seg_ref[...].astype(F32)
        k = iota((LOC, WINDOW), 1)
        q = iota((LOC, WINDOW), 0)
        allowed = (k <= q + REACH) & (k >= REACH - ctx * LOC) & (key_seg == query_seg)
        bias[...] = jnp.where(allowed, F32(0), F32(-1e30))

    if packed:
        queries[...] = jnp.dot(hot_ref[core], q_ref[...], preferred_element_type=F32).astype(BF16)
    else:
        queries[...] = q_ref[...]
    columns = pl.ds(pl.multiple_of(head * HEAD_SIZE, HEAD_SIZE), HEAD_SIZE)
    key_rows = keys[:, columns]
    value_rows = values[:, columns]
    value_rows = jnp.concatenate([value_rows, jnp.ones_like(value_rows)], axis=1)
    for g in range(HEAD_GROUP):
        cols = slice(g * HEAD_SIZE, (g + 1) * HEAD_SIZE)
        scores = lax.dot_general(
            queries[:, cols], key_rows, (((1,), (1,)), ((), ())), preferred_element_type=F32
        )
        scores = scores + bias[...]
        best = jnp.max(scores, axis=-1, keepdims=True)
        p = jnp.exp2((scores - best) * SCORE_BASE2).astype(BF16)
        summed = jnp.dot(p, value_rows, preferred_element_type=F32)
        out_ref[:, cols] = (summed[:, :HEAD_SIZE] / summed[:, HEAD_SIZE:]).astype(BF16)


def attend(where, seg_col, hots, queries, part, mine, other, start):
    heads = KEY_VALUE_HEADS // 2
    packed = queries.shape[0] == SLOTS
    first = 0 if part * heads < EARLY else EARLY
    return pl.pallas_call(
        functools.partial(attend_kernel, packed),
        grid=(heads,),
        in_specs=[
            pl.BlockSpec(memory_space=pltpu.SMEM),
            whole((LOC, 1)),
            whole((2, LOC, SLOTS)),
            pl.BlockSpec((queries.shape[0], GROUP_WIDTH), lambda i: (0, part * heads - first + i)),
        ]
        + [pl.BlockSpec((SENT, HALF), lambda i: (0, part))] * 6
        + [pl.BlockSpec(memory_space=pl.ANY)] * len(start),
        out_specs=pl.BlockSpec((LOC, GROUP_WIDTH), lambda i: (0, part * heads + i)),
        out_shape=jax.ShapeDtypeStruct((LOC, QUERY_WIDTH), BF16),
        input_output_aliases={10: 0} if start else {},
        scratch_shapes=[
            pltpu.VMEM((WINDOW, HALF), BF16),
            pltpu.VMEM((WINDOW, HALF), BF16),
            pltpu.VMEM((LOC, WINDOW), F32),
            pltpu.VMEM((LOC, GROUP_WIDTH), BF16),
        ],
        compiler_params=pltpu.CompilerParams(**PARAMS),
        cost_estimate=pl.CostEstimate(
            flops=2 * LOC * WINDOW * QUERY_WIDTH,
            bytes_accessed=4 << 20,
            transcendentals=LOC * WINDOW * QUERY_HEADS // 2,
        ),
        name="attend",
    )(where, seg_col, hots, queries, *mine, *other, *start)


def chips():
    return [(x, y, z, k) for x in range(4) for z in range(8) for y in range(4) for k in range(2)]


def device(x, y, z, k):
    return (x % 4 * 8 + z % 8) * 8 + y % 4 * 2 + k


def shift(array, moved):
    pairs = [(device(*c), device(*moved(*c))) for c in chips()]
    return lax.ppermute(array, ("dp", "ctx"), pairs)


def swap_cores(array):
    return shift(array, lambda x, y, z, k: (x, y, z, 1 - k))


def send_up(array, by):
    pairs = [(device(*c), device(c[0], c[1] + by, c[2], c[3])) for c in chips() if c[1] + by < 4]
    return lax.ppermute(array, ("dp", "ctx"), pairs)


def along_z(array):
    groups = [[device(x, y, z, k) for z in range(8)] for x in range(4) for y in range(4) for k in range(2)]
    copies = jnp.broadcast_to(array[None], (8,) + array.shape)
    got = lax.all_to_all(copies, ("dp", "ctx"), 0, 0, axis_index_groups=groups, tiled=True)
    return got.reshape(8 * array.shape[0], array.shape[1])


def along_first(array, by):
    return shift(array, lambda x, y, z, k: (x + by, y, z, k) if k == 0 else (x, y + by, z, k))


def along_second(array, by):
    return shift(array, lambda x, y, z, k: (x, y + by, z, k) if k == 0 else (x + by, y, z, k))


def move(slots, rows):
    width = slots.shape[1]
    sent = slots.reshape(RANKS, rows, width)
    return lax.all_to_all(sent, "dp", split_axis=0, concat_axis=0, tiled=True).reshape(RANKS * rows, width)


def body(gen_rows, gen_queries, place, segment, key_value_weight, key_norm_gain):
    ctx = lax.axis_index("ctx")
    core, chip_y = ctx % 2, ctx // 2
    chip_x = lax.axis_index("dp") // 8
    where = jnp.stack([core, chip_x, chip_y, ctx])
    core_s = core.reshape(1)
    seg = segment.reshape(LOC)
    col, row = place.reshape(LOC, 1), place.reshape(1, LOC)

    part = lax.dynamic_slice_in_dim(
        key_value_weight, core * ROW_WIDTH + chip_y * HEAD_SIZE, HEAD_SIZE, 1
    )
    run = along_z(part)
    (early_slots, late_slots), run = lax.optimization_barrier((pack_queries(col, row, gen_queries), run))
    near = jnp.concatenate([run, along_first(run, 1)])
    far = jnp.concatenate([along_first(run, -1), along_first(run, 2)])
    early_slots, near, far = lax.optimization_barrier((early_slots, near, far))
    got_early = move(early_slots, CAPACITY)

    sib = swap_cores(jnp.stack([place, seg]))
    sib_rows = swap_cores(gen_rows)
    sib_col, sib_row = sib[0].reshape(LOC, 1), sib[0].reshape(1, LOC)
    pair_seg = jnp.where(core == 0, jnp.concatenate([seg, sib[1]]), jnp.concatenate([sib[1], seg]))
    pair_seg = pair_seg.reshape(1, PAIR)

    below, below_far = along_second(near, 1), along_second(far, 1)
    above, above_far = along_second(near, -1), along_second(far, -1)
    opposite, opposite_far = along_second(above, -1), along_second(below_far, 1)
    weights = [near, far, below, below_far, above, above_far, opposite, opposite_far]
    hot = row_places(core_s, col, row, sib_col, sib_row)
    offsets = jnp.array(NEAR)
    table = jnp.concatenate([(chip_x + offsets) % 4, (chip_y + offsets) % 4, core_s])
    slots = project(table, hot, key_norm_gain.reshape(1, ROW_WIDTH), gen_rows, sib_rows, weights)
    slots, got_early = lax.optimization_barrier((slots, got_early))
    got = move(slots, 2 * CAPACITY)
    own_code = got_early[:, EARLY * GROUP_WIDTH :]
    hots = places(core_s, own_code, swap_cores(own_code))
    early = unpack_queries(core_s, hots, got_early, EARLY)
    got, early, hots = lax.optimization_barrier((got, early, hots))
    own = unpack(hots, pair_seg, got)
    late_slots, own = lax.optimization_barrier((late_slots, own))
    up = [send_up(own, 1), send_up(own, 2)]
    got_late = move(late_slots, CAPACITY)
    other = [swap_cores(m) for m in [own] + up]
    seg_col = seg.reshape(LOC, 1)
    mine = [own] + up
    out = attend(where, seg_col, hots, early, 0, mine, other, [])
    got_late, out = lax.optimization_barrier((got_late, out))
    return attend(where, seg_col, hots, got_late, 1, mine, other, [out])


def solution(mesh):
    placed = (
        P(("dp", "ctx"), None),
        P(("dp", "ctx"), None),
        P(("dp", "ctx")),
        P("dp", "ctx"),
        P("dp", None),
        P(),
    )
    return jax.shard_map(
        body, mesh=mesh, in_specs=placed, out_specs=P(("dp", "ctx"), None), check_vma=False
    )
```
